32 devices in a mesh: ty: 8 (over y, x, core), tx: 4 (over z).
Axes of the slice: x: 2, y: 2, z: 4, core: 2. Of those that a mesh axis runs over, the one named last changes fastest.
Arguments:
- object_field: float32 [2, 2048, 1024], P(None, 'ty', 'tx'), may hold values from -6 to 6
- probe_modes: float32 [2, 2, 256, 256], replicated, may hold values from -6 to 6
- intensities: float32 [8, 4, 3, 256, 256], P('ty', 'tx'), may hold values from 0.25 to 16
- offsets: int32 [8, 4, 3, 2], P('ty', 'tx'), may hold values from 0 to 256
- counts: int32 [8, 4], replicated, may hold values from 1 to 3, as said below
Outputs:
- object_grad: float32 [2, 2048, 1024], P(None, 'ty', 'tx')
- probe_grad: float32 [2, 2, 256, 256], replicated
The draws below stay inside these ranges and needn't reach their ends.
Inputs may be any that keep to these rules, and one draw needn't show every extreme that they name: Tile (a, b) uses slots 0 to counts[a, b] - 1 of intensities and offsets; its other slots are ignored. In every draw some tile uses all 3 slots.
All inputs are finite; a program needn't handle non-finite values.
Results may differ from the reference program's by a relative error of at most 0.0003.
Values sent between devices are 32-bit elements; how exact they have to be, the bound alone decides.
No kernel may reach another device: no remote copies, remote signals or barrier semaphores. Data moves between devices by JAX's collectives and lax.ppermute only.
A program may use at most 64 MiB of HBM per device.

```python
import jax
import jax.numpy as jnp
from jax import lax

P_SIZE = 256
MODES = 2
TILE = 256
CAP = 3
NY = 2048
NX = 1024
N_TY = 8
N_TX = 4


def draw_counts(key, part):
    first_key, second_key = jax.random.split(key)
    levels = jax.random.randint(first_key, (N_TY * N_TX,), 0, 65)
    listed = 1 + (CAP - 1) * levels * levels // 4096
    chosen = jax.random.randint(second_key, (), 0, N_TY * N_TX)
    listed = jnp.where(jnp.arange(N_TY * N_TX, dtype=jnp.int32) == chosen, CAP, listed)
    return listed.reshape(N_TY, N_TX).astype(jnp.int32)


def place_ends(result, own_key, smallest, top_value):
    place = [jax.random.randint(jax.random.fold_in(own_key, axis), (), 0, length) for axis, length in enumerate(result.shape)]
    widest = result.shape.index(max(result.shape))
    neighbour = place[:widest] + [(place[widest] + 1) % result.shape[widest]] + place[widest + 1:]
    return result.at[tuple(place)].set(smallest).at[tuple(neighbour)].set(top_value)


def steps_of(stream_key, extent, cuts, low, high):
    loudness = 1.0
    for position, shards_of in cuts:
        heights = jax.random.uniform(jax.random.fold_in(jax.random.fold_in(stream_key, 6), position), (shards_of,), jnp.float32, low / len(cuts), high / len(cuts))
        loudness = loudness * jnp.repeat(jnp.exp(heights), extent[position] // shards_of).reshape((-1,) + (1,) * (len(extent) - 1 - position))
    return loudness


def gaussian(stream_key, extent, scale, bound, cuts=(), kind=jnp.bfloat16):
    values = jax.random.normal(stream_key, extent, jnp.float32) * scale
    if len(cuts) > 0:
        values = steps_of(stream_key, extent, cuts, -0.22, 0.18) * values
    return jnp.clip(values, min=-bound, max=bound).astype(kind)


def setup_inputs(seed: int = 0) -> dict:
    key_of = jax.random.split(jax.random.key(seed), 6)
    return {
        "object_field": gaussian(key_of[0], (2, NY, NX), 1.0, 6.0, ((1, 8), (2, 4)), jnp.float32),
        "probe_modes": gaussian(key_of[1], (2, MODES, P_SIZE, P_SIZE), 0.7, 6.0, (), jnp.float32),
        "intensities": jnp.clip(0.25 + 15.75 * jax.random.uniform(key_of[2], (N_TY, N_TX, CAP, P_SIZE, P_SIZE), jnp.float32) ** steps_of(key_of[2], (N_TY, N_TX, CAP, P_SIZE, P_SIZE), ((0, 8), (1, 4)), -0.2, 0.2), 0.25, 16.0),
        "offsets": place_ends(jax.random.randint(key_of[3], (N_TY, N_TX, CAP, 2), 0, TILE + 1), jax.random.fold_in(key_of[3], 1), 0, TILE).astype(jnp.int32),
        "counts": draw_counts(jax.random.fold_in(key_of[5], 71), 0),
    }


FLOOR = 0.5

def reference(object_field, probe_modes, intensities, offsets, counts):
    margin = P_SIZE // 2
    padded = jnp.pad(object_field, ((0, 0), (margin, margin), (margin, margin)))
    complex_object = padded[0] + 1j * padded[1]
    probe = probe_modes[0] + 1j * probe_modes[1]
    total_slots = N_TY * N_TX * CAP

    def visit(carry, slot_index):
        grid, probe_sum = carry
        tile_row = (slot_index // (N_TX * CAP)).astype(jnp.int32)
        tile_col = (slot_index // CAP % N_TX).astype(jnp.int32)
        within = (slot_index % CAP).astype(jnp.int32)
        weight = (within < counts[tile_row, tile_col]).astype(jnp.float32)
        row_start = (tile_row * TILE + offsets[tile_row, tile_col, within, 0]).astype(jnp.int32)
        col_start = (tile_col * TILE + offsets[tile_row, tile_col, within, 1]).astype(jnp.int32)
        patch = lax.dynamic_slice(complex_object, (row_start, col_start), (P_SIZE, P_SIZE))
        far_field = jnp.fft.fft2(probe * patch, norm='ortho')
        amplitude = jnp.sqrt(lax.optimization_barrier(jnp.sum(jnp.real(far_field) * jnp.real(far_field) + jnp.imag(far_field) * jnp.imag(far_field), axis=0)))
        factor = 1.0 - jnp.sqrt(intensities[tile_row, tile_col, within]) / jnp.maximum(amplitude, FLOOR)
        backward = jnp.fft.ifft2(far_field * factor, norm='ortho')
        object_part = lax.optimization_barrier(jnp.sum(jnp.conj(probe) * backward, axis=0)) * weight
        current = lax.dynamic_slice(grid, (row_start, col_start), (P_SIZE, P_SIZE))
        grid = lax.dynamic_update_slice(grid, current + object_part, (row_start, col_start))
        probe_sum = probe_sum + jnp.conj(patch) * backward * weight
        return ((grid, probe_sum), None)
    start_carry = (jnp.zeros_like(complex_object), jnp.zeros_like(probe))
    (grid, probe_sum), _ = lax.scan(visit, start_carry, jnp.arange(total_slots, dtype=jnp.int32))
    inner = grid[margin:-margin, margin:-margin]
    object_grad = jnp.stack([jnp.real(inner), jnp.imag(inner)]).astype(jnp.float32)
    probe_total = probe_sum / (N_TY * N_TX)
    probe_grad = jnp.stack([jnp.real(probe_total), jnp.imag(probe_total)]).astype(jnp.float32)
    return (object_grad, probe_grad)
```

```python
import functools
import math

import jax
import jax.numpy as jnp
import ml_dtypes
import numpy as np
from jax import lax
from jax.experimental import pallas as pl
from jax.experimental.pallas import tpu as pltpu
from jax.sharding import PartitionSpec as P

FLOOR = 0.5
LANES = 128
CHUNK = 32
VMEM_LIMIT = 40 * 1024 * 1024


def split_table(table):
    high = table.astype(ml_dtypes.bfloat16)
    low = (table - high.astype(np.float64)).astype(ml_dtypes.bfloat16)
    return high, low


def complex_block(matrix):
    return np.block([[matrix.real, matrix.imag], [-matrix.imag, matrix.real]])


@functools.lru_cache(maxsize=None)
def fourier_tables(pattern):
    half = pattern // 2
    n = np.arange(half)
    tables = []
    for parity in (0, 1):
        k = 2 * np.arange(half) + parity
        tables.append(np.exp(-2j * np.pi * ((n[:, None] * k[None, :]) % pattern) / pattern) / math.sqrt(pattern))
    forward = [complex_block(t) for t in tables]
    inverse = [complex_block(np.conj(t).T) for t in tables]
    every = forward + [t.T for t in forward] + [t.T for t in inverse] + inverse
    return np.stack([np.stack(split_table(t)) for t in every])


def split(value):
    high = value.astype(jnp.bfloat16)
    low = (value - high.astype(jnp.float32)).astype(jnp.bfloat16)
    return high, low


def mul(a, b):
    return jnp.dot(a, b, preferred_element_type=jnp.float32)


def slots_kernel(
    scalars, spots, center, left, right, above, below, probe, root, tables,
    grad_left, grad_mid, grad_right, probe_out,
    pad, grid, patch, rows_high, rows_low, freq, sums,
):
    half = LANES
    modes = probe.shape[1]
    length = center.shape[1]
    margin = left.shape[2]
    top, bottom = slice(0, half), slice(half, 2 * half)

    pad[:, 0, margin : margin + length, :] = left[...]
    pad[:, 3, margin : margin + length, :] = right[...]
    for b in range(2):
        pad[:, 1 + b, margin : margin + length, :] = center[:, :, b * half : (b + 1) * half]
    for b in range(4):
        pad[:, b, :margin, :] = above[:, :, b * half : (b + 1) * half]
        pad[:, b, margin + length :, :] = below[:, :, b * half : (b + 1) * half]
    grid[...] = jnp.zeros_like(grid)
    sums[...] = jnp.zeros_like(sums)
    lane = lax.broadcasted_iota(jnp.int32, (CHUNK, half), 1)

    def slot_step(slot, carry):
        row0 = spots[slot, 0]
        col0 = spots[slot, 1]
        block = jnp.minimum(col0 // half, 1)
        shift = col0 - block * half
        back_shift = lax.rem(half - shift, half)
        fore_shift = lax.rem(shift, half)

        for chunk in range(half // CHUNK):
            spectra = []
            for part in range(2):
                rows = part * half + chunk * CHUNK
                here = slice(rows, rows + CHUNK)
                cells = []
                for c in range(2):
                    rolled = [
                        pltpu.roll(pad[c, block + b, pl.ds(row0 + rows, CHUNK), :], back_shift, 1) for b in range(3)
                    ]
                    for b in range(2):
                        cell = jnp.where(lane < half - shift, rolled[b], rolled[b + 1])
                        patch[c, b, here, :] = cell
                        cells.append(cell)
                lefts = []
                for m in range(modes):
                    waves = []
                    for b in range(2):
                        pr = probe[0, m, here, b * half : (b + 1) * half]
                        pi = probe[1, m, here, b * half : (b + 1) * half]
                        waves.append((pr * cells[b] - pi * cells[2 + b], pr * cells[2 + b] + pi * cells[b]))
                    (ra, ia), (rb, ib) = waves
                    lefts.append((jnp.concatenate([ra + rb, ia + ib], axis=1), jnp.concatenate([ra - rb, ia - ib], axis=1)))
                spectra.append(lefts)
            for parity in range(2):
                stacked = jnp.concatenate([spectra[part][m][parity] for m in range(modes) for part in range(2)], axis=0)
                high, low = split(stacked)
                out = mul(high, tables[parity, 0]) + (mul(low, tables[parity, 0]) + mul(high, tables[parity, 1]))
                for m in range(modes):
                    a = out[(2 * m) * CHUNK : (2 * m + 1) * CHUNK]
                    b = out[(2 * m + 1) * CHUNK : (2 * m + 2) * CHUNK]
                    for row_parity, value in enumerate((a + b, a - b)):
                        vh, vl = split(value)
                        for c in range(2):
                            at = slice(c * half + chunk * CHUNK, c * half + (chunk + 1) * CHUNK)
                            to = slice(parity * half, (parity + 1) * half)
                            rows_high[m, row_parity, at, to] = vh[:, c * half : (c + 1) * half]
                            rows_low[m, row_parity, at, to] = vl[:, c * half : (c + 1) * half]

        def row_transform(table):
            for m in range(modes):
                for parity in range(2):
                    high = rows_high[m, parity]
                    low = rows_low[m, parity]
                    freq[m, parity] = mul(tables[table + parity, 0], high) + (
                        mul(tables[table + parity, 1], high) + mul(tables[table + parity, 0], low)
                    )

        row_transform(2)

        for parity in range(2):
            for chunk in range(half // CHUNK):
                real = slice(chunk * CHUNK, (chunk + 1) * CHUNK)
                imag = slice(half + chunk * CHUNK, half + (chunk + 1) * CHUNK)
                values = [(freq[m, parity, real, :], freq[m, parity, imag, :]) for m in range(modes)]
                power = sum(re * re + im * im for re, im in values)
                factor = 1.0 - root[slot, parity, real, :] * lax.rsqrt(jnp.maximum(power, FLOOR * FLOOR))
                for m in range(modes):
                    for at, value in zip((real, imag), values[m]):
                        vh, vl = split(value * factor)
                        rows_high[m, parity, at, :] = vh
                        rows_low[m, parity, at, :] = vl

        row_transform(4)

        for chunk in range(half // CHUNK):
            real = slice(chunk * CHUNK, (chunk + 1) * CHUNK)
            imag = slice(half + chunk * CHUNK, half + (chunk + 1) * CHUNK)
            backs = []
            for q in range(2):
                cols = slice(q * half, (q + 1) * half)
                pieces = []
                for m in range(modes):
                    even = jnp.concatenate([freq[m, 0, real, cols], freq[m, 0, imag, cols]], axis=1)
                    odd = jnp.concatenate([freq[m, 1, real, cols], freq[m, 1, imag, cols]], axis=1)
                    pieces += [even + odd, even - odd]
                high, low = split(jnp.concatenate(pieces, axis=0))
                backs.append(mul(high, tables[6 + q, 0]) + (mul(low, tables[6 + q, 0]) + mul(high, tables[6 + q, 1])))
            halves = (backs[0] + backs[1], backs[0] - backs[1])
            for part in range(2):
                rows = part * half + chunk * CHUNK
                here = slice(rows, rows + CHUNK)
                total = [[0.0, 0.0], [0.0, 0.0]]
                for b in range(2):
                    xr = patch[0, b, here, :]
                    xi = patch[1, b, here, :]
                    for m in range(modes):
                        at = (2 * m + part) * CHUNK
                        br = halves[b][at : at + CHUNK, :half]
                        bi = halves[b][at : at + CHUNK, half:]
                        pr = probe[0, m, here, b * half : (b + 1) * half]
                        pi = probe[1, m, here, b * half : (b + 1) * half]
                        total[0][b] += pr * br + pi * bi
                        total[1][b] += pr * bi - pi * br
                        sums[b, 0, m, here, :] += xr * br + xi * bi
                        sums[b, 1, m, here, :] += xr * bi - xi * br
                for c in range(2):
                    ra = pltpu.roll(total[c][0], fore_shift, 1)
                    rb = pltpu.roll(total[c][1], fore_shift, 1)
                    beyond = lane >= shift
                    zero = jnp.zeros_like(ra)
                    placed = (jnp.where(beyond, ra, zero), jnp.where(beyond, rb, ra), jnp.where(beyond, zero, rb))
                    for b in range(3):
                        grid[c, block + b, pl.ds(row0 + rows, CHUNK), :] += placed[b]
        return carry

    lax.fori_loop(0, scalars[0], slot_step, 0)

    grad_left[...] = grid[:, 0]
    grad_right[...] = grid[:, 3]
    for b in range(2):
        grad_mid[:, :, b * half : (b + 1) * half] = grid[:, 1 + b]
    pieces, rows, _ = probe_out.shape
    code = scalars[1]
    for b in range(2):
        for c in range(2):
            for m in range(modes):
                first = ((b * 2 + c) * modes + m) * length
                for at in range(0, length, rows):
                    probe_out[(first + at) // rows ^ code] = sums[b, c, m, at : at + rows, :]


def join_kernel(scalars, ordered, out):
    pieces, rows, _ = ordered.shape
    _, modes, length, _ = out.shape
    code = scalars[1]
    for b in range(2):
        for c in range(2):
            for m in range(modes):
                first = ((b * 2 + c) * modes + m) * length
                for at in range(0, length, rows):
                    out[c, m, at : at + rows, b * LANES : (b + 1) * LANES] = ordered[(first + at) // rows ^ code]


def shifted(value, axis, steps):
    count = lax.axis_size(axis)
    initial, last = (max(0, -steps), min(count, count - steps))
    return lax.ppermute(value, axis, [(source, source + steps) for source in range(initial, last)])


def exchanged(value, axis, mask):
    return lax.ppermute(value, axis, [(i, i ^ mask) for i in range(lax.axis_size(axis))])


def digit_groups():
    groups = [("ty", [1])]
    for axis, first in (("ty", 1), ("tx", 0)):
        bits = [1 << i for i in range(first, lax.axis_size(axis).bit_length() - 1)]
        groups += [(axis, bits[i : i + 2]) for i in range(0, len(bits), 2)]
    return groups


def masks(bits):
    return [sum(bit for i, bit in enumerate(reversed(bits)) if j >> i & 1) for j in range(1 << len(bits))]


def own_code(groups):
    code = 0
    for axis, bits in groups:
        index = lax.axis_index(axis)
        for bit in bits:
            code = code * 2 + (index // bit) % 2
    return code


def sum_everywhere(value, groups, scale):
    for axis, bits in groups:
        places = masks(bits)
        count = value.shape[0] // len(places)
        taken = [exchanged(value[j * count : (j + 1) * count], axis, places[j]) for j in range(1, len(places))]
        value = value[:count] + sum(taken[1:], taken[0])
    value = value * scale
    for axis, bits in reversed(groups):
        value = jnp.concatenate([value] + [exchanged(value, axis, mask) for mask in masks(bits)[1:]], axis=0)
    return value


def shards(object_field, probe_modes, intensities, offsets, counts):
    length = object_field.shape[1]
    modes, pattern = probe_modes.shape[1:3]
    margin = pattern // 2
    half = LANES
    devices = lax.axis_size("ty") * lax.axis_size("tx")
    groups = digit_groups()
    vmem = pl.BlockSpec(memory_space=pltpu.VMEM)
    smem = pl.BlockSpec(memory_space=pltpu.SMEM)
    params = pltpu.CompilerParams(vmem_limit_bytes=VMEM_LIMIT)

    left = shifted(object_field[:, :, length - margin :], "tx", 1)
    right = shifted(object_field[:, :, :margin], "tx", -1)
    wide = jnp.concatenate([left, object_field, right], axis=2)
    above = shifted(wide[:, length - margin :, :], "ty", 1)
    below = shifted(wide[:, :margin, :], "ty", -1)

    listed = counts[lax.axis_index("ty"), lax.axis_index("tx")]
    scalars = jnp.stack([listed, own_code(groups)]).astype(jnp.int32)
    slots = intensities.shape[2]
    root = jnp.sqrt(intensities[0, 0]).reshape(slots, half, 2, half, 2).transpose(0, 2, 1, 4, 3).reshape(slots, 2, half, pattern)
    tables = jnp.asarray(fourier_tables(pattern))
    rows = 2 * 2 * modes * pattern // devices
    f32, bf16 = jnp.float32, jnp.bfloat16
    grad_left, grad_mid, grad_right, probe_part = pl.pallas_call(
        slots_kernel,
        out_shape=(
            jax.ShapeDtypeStruct((2, length + 2 * margin, margin), f32),
            jax.ShapeDtypeStruct((2, length + 2 * margin, length), f32),
            jax.ShapeDtypeStruct((2, length + 2 * margin, margin), f32),
            jax.ShapeDtypeStruct((devices, rows, half), f32),
        ),
        in_specs=[smem, smem] + [vmem] * 8,
        out_specs=(vmem,) * 4,
        scratch_shapes=[
            pltpu.VMEM((2, 4, length + 2 * margin, half), f32),
            pltpu.VMEM((2, 4, length + 2 * margin, half), f32),
            pltpu.VMEM((2, 2, pattern, half), f32),
            pltpu.VMEM((modes, 2, pattern, pattern), bf16),
            pltpu.VMEM((modes, 2, pattern, pattern), bf16),
            pltpu.VMEM((modes, 2, pattern, pattern), f32),
            pltpu.VMEM((2, 2, modes, pattern, half), f32),
        ],
        compiler_params=params,
        name="slots",
    )(scalars, offsets[0, 0], object_field, left, right, above, below, probe_modes, root, tables)

    from_right = shifted(grad_left, "tx", -1)
    from_left = shifted(grad_right, "tx", 1)
    middle = grad_mid + jnp.concatenate([from_left, from_right], axis=2)
    from_below = shifted(middle[:, :margin, :], "ty", -1)
    from_above = shifted(middle[:, margin + length :, :], "ty", 1)
    inner = middle[:, margin : margin + length, :] + jnp.concatenate([from_above, from_below], axis=1)

    ordered = sum_everywhere(probe_part, groups, 1.0 / devices)
    probe_grad = pl.pallas_call(
        join_kernel,
        out_shape=jax.ShapeDtypeStruct(probe_modes.shape, f32),
        in_specs=[smem, vmem],
        out_specs=vmem,
        compiler_params=params,
        name="join",
    )(scalars, ordered)
    return (inner, probe_grad)


def solution(mesh):
    placed = (
        P(None, "ty", "tx"),
        P(),
        P("ty", "tx", None, None, None),
        P("ty", "tx", None, None),
        P(),
    )
    return jax.shard_map(
        shards, mesh=mesh, in_specs=placed, out_specs=(P(None, "ty", "tx"), P()), check_vma=False
    )
```

```python
import functools
import math

import jax
import jax.numpy as jnp
import ml_dtypes
import numpy as np
from jax import lax
from jax.experimental import pallas as pl
from jax.experimental.pallas import tpu as pltpu
from jax.sharding import PartitionSpec as P

FLOOR = 0.5
LANES = 128
CHUNK = 32
VMEM_LIMIT = 28 * 1024 * 1024
SMALL_LIMIT = 8 * 1024 * 1024


def split_table(table):
    high = table.astype(ml_dtypes.bfloat16)
    low = (table - high.astype(np.float64)).astype(ml_dtypes.bfloat16)
    return high, low


def complex_block(matrix):
    return np.block([[matrix.real, matrix.imag], [-matrix.imag, matrix.real]])


@functools.lru_cache(maxsize=None)
def fourier_tables(pattern):
    half = pattern // 2
    n = np.arange(half)
    tables = []
    for parity in (0, 1):
        k = 2 * np.arange(half) + parity
        tables.append(np.exp(-2j * np.pi * ((n[:, None] * k[None, :]) % pattern) / pattern) / math.sqrt(pattern))
    forward = [complex_block(t) for t in tables]
    inverse = [complex_block(np.conj(t).T) for t in tables]
    every = forward + [t.T for t in forward] + [t.T for t in inverse] + inverse
    return np.stack([np.stack(split_table(t)) for t in every])


@functools.lru_cache(maxsize=None)
def column_order(pattern):
    return np.eye(pattern)[:, np.r_[0:pattern:2, 1:pattern:2]].astype(ml_dtypes.bfloat16)


def split(value):
    high = value.astype(jnp.bfloat16)
    low = (value - high.astype(jnp.float32)).astype(jnp.bfloat16)
    return high, low


def mul(a, b):
    return jnp.dot(a, b, preferred_element_type=jnp.float32)


def edges_kernel(center, to_right, to_left, to_core, to_chip):
    half = LANES
    to_right[...] = center[:, :, half:]
    to_left[...] = center[:, :, :half]
    odd = lax.axis_index("ty") % 2
    near = pl.multiple_of((1 - odd) * half, half)
    far = pl.multiple_of(odd * half, half)
    to_core[...] = center[:, pl.ds(near, half), :]
    to_chip[...] = center[:, pl.ds(far, half), :]


def corners_kernel(left, right, to_core, to_chip):
    half = LANES
    odd = lax.axis_index("ty") % 2
    near = pl.multiple_of((1 - odd) * half, half)
    far = pl.multiple_of(odd * half, half)
    for side, cols in enumerate((left, right)):
        to_core[side] = cols[:, pl.ds(near, half), :]
        to_chip[side] = cols[:, pl.ds(far, half), :]


def root_kernel(measured, order, root, halves):
    for slot in range(measured.shape[0]):
        for b in range(2):
            halves[slot, b] = jnp.sqrt(measured[slot, :, b * LANES : (b + 1) * LANES])
        for parity in range(2):
            rows = pl.ds(parity, LANES, stride=2)
            high, low = split(jnp.concatenate([halves[slot, 0, rows, :], halves[slot, 1, rows, :]], axis=1))
            root[slot, parity] = mul(high, order[...]) + mul(low, order[...])


def slots_kernel(
    counts, spots, center, left, right, core_rows, chip_rows, core_corners, chip_corners, probe, root, tables,
    core_out, chip_out, grad_mid, probe_keep,
    pad, grid, patch, rows_high, rows_low, freq, sums,
):
    half = LANES
    modes = probe.shape[1]
    length = center.shape[1]
    margin = left.shape[2]
    odd = lax.axis_index("ty") % 2
    near = pl.multiple_of((1 - odd) * (margin + length), half)
    far = pl.multiple_of(odd * (margin + length), half)

    pad[:, 0, margin : margin + length, :] = left[...]
    pad[:, 3, margin : margin + length, :] = right[...]
    for b in range(2):
        cols = slice(b * half, (b + 1) * half)
        pad[:, 1 + b, margin : margin + length, :] = center[:, :, cols]
        for start, rows, corners in ((near, core_rows, core_corners), (far, chip_rows, chip_corners)):
            pad[:, 1 + b, pl.ds(start, margin), :] = rows[:, :, cols]
            pad[:, 3 * b, pl.ds(start, margin), :] = corners[b]
    grid[...] = jnp.zeros_like(grid)
    sums[...] = jnp.zeros_like(sums)
    lane = lax.broadcasted_iota(jnp.int32, (CHUNK, half), 1)

    def slot_step(slot, carry):
        row0 = spots[slot, 0]
        col0 = spots[slot, 1]
        block = jnp.minimum(col0 // half, 1)
        shift = col0 - block * half
        back_shift = lax.rem(half - shift, half)
        fore_shift = lax.rem(shift, half)

        for chunk in range(half // CHUNK):
            spectra = []
            for part in range(2):
                rows = part * half + chunk * CHUNK
                here = slice(rows, rows + CHUNK)
                cells = []
                for c in range(2):
                    rolled = [
                        pltpu.roll(pad[c, block + b, pl.ds(row0 + rows, CHUNK), :], back_shift, 1) for b in range(3)
                    ]
                    for b in range(2):
                        cell = jnp.where(lane < half - shift, rolled[b], rolled[b + 1])
                        patch[c, b, here, :] = cell
                        cells.append(cell)
                lefts = []
                for m in range(modes):
                    waves = []
                    for b in range(2):
                        pr = probe[0, m, here, b * half : (b + 1) * half]
                        pi = probe[1, m, here, b * half : (b + 1) * half]
                        waves.append((pr * cells[b] - pi * cells[2 + b], pr * cells[2 + b] + pi * cells[b]))
                    (ra, ia), (rb, ib) = waves
                    lefts.append((jnp.concatenate([ra + rb, ia + ib], axis=1), jnp.concatenate([ra - rb, ia - ib], axis=1)))
                spectra.append(lefts)
            for parity in range(2):
                stacked = jnp.concatenate([spectra[part][m][parity] for m in range(modes) for part in range(2)], axis=0)
                high, low = split(stacked)
                out = mul(high, tables[parity, 0]) + (mul(low, tables[parity, 0]) + mul(high, tables[parity, 1]))
                for m in range(modes):
                    a = out[(2 * m) * CHUNK : (2 * m + 1) * CHUNK]
                    b = out[(2 * m + 1) * CHUNK : (2 * m + 2) * CHUNK]
                    for row_parity, value in enumerate((a + b, a - b)):
                        vh, vl = split(value)
                        for c in range(2):
                            at = slice(c * half + chunk * CHUNK, c * half + (chunk + 1) * CHUNK)
                            to = slice(parity * half, (parity + 1) * half)
                            rows_high[m, row_parity, at, to] = vh[:, c * half : (c + 1) * half]
                            rows_low[m, row_parity, at, to] = vl[:, c * half : (c + 1) * half]

        def row_transform(table):
            for m in range(modes):
                for parity in range(2):
                    high = rows_high[m, parity]
                    low = rows_low[m, parity]
                    freq[m, parity] = mul(tables[table + parity, 0], high) + (
                        mul(tables[table + parity, 1], high) + mul(tables[table + parity, 0], low)
                    )

        row_transform(2)

        for parity in range(2):
            for chunk in range(half // CHUNK):
                real = slice(chunk * CHUNK, (chunk + 1) * CHUNK)
                imag = slice(half + chunk * CHUNK, half + (chunk + 1) * CHUNK)
                values = [(freq[m, parity, real, :], freq[m, parity, imag, :]) for m in range(modes)]
                power = sum(re * re + im * im for re, im in values)
                factor = 1.0 - root[slot, parity, real, :] * lax.rsqrt(jnp.maximum(power, FLOOR * FLOOR))
                for m in range(modes):
                    for at, value in zip((real, imag), values[m]):
                        vh, vl = split(value * factor)
                        rows_high[m, parity, at, :] = vh
                        rows_low[m, parity, at, :] = vl

        row_transform(4)

        for chunk in range(half // CHUNK):
            real = slice(chunk * CHUNK, (chunk + 1) * CHUNK)
            imag = slice(half + chunk * CHUNK, half + (chunk + 1) * CHUNK)
            backs = []
            for q in range(2):
                cols = slice(q * half, (q + 1) * half)
                pieces = []
                for m in range(modes):
                    even = jnp.concatenate([freq[m, 0, real, cols], freq[m, 0, imag, cols]], axis=1)
                    odd = jnp.concatenate([freq[m, 1, real, cols], freq[m, 1, imag, cols]], axis=1)
                    pieces += [even + odd, even - odd]
                high, low = split(jnp.concatenate(pieces, axis=0))
                backs.append(mul(high, tables[6 + q, 0]) + (mul(low, tables[6 + q, 0]) + mul(high, tables[6 + q, 1])))
            halves = (backs[0] + backs[1], backs[0] - backs[1])
            for part in range(2):
                rows = part * half + chunk * CHUNK
                here = slice(rows, rows + CHUNK)
                total = [[0.0, 0.0], [0.0, 0.0]]
                for b in range(2):
                    xr = patch[0, b, here, :]
                    xi = patch[1, b, here, :]
                    for m in range(modes):
                        at = (2 * m + part) * CHUNK
                        br = halves[b][at : at + CHUNK, :half]
                        bi = halves[b][at : at + CHUNK, half:]
                        pr = probe[0, m, here, b * half : (b + 1) * half]
                        pi = probe[1, m, here, b * half : (b + 1) * half]
                        total[0][b] += pr * br + pi * bi
                        total[1][b] += pr * bi - pi * br
                        sums[pl.ds(((b * 2 + 0) * modes + m) * length + rows, CHUNK), :] += xr * br + xi * bi
                        sums[pl.ds(((b * 2 + 1) * modes + m) * length + rows, CHUNK), :] += xr * bi - xi * br
                for c in range(2):
                    ra = pltpu.roll(total[c][0], fore_shift, 1)
                    rb = pltpu.roll(total[c][1], fore_shift, 1)
                    beyond = lane >= shift
                    zero = jnp.zeros_like(ra)
                    placed = (jnp.where(beyond, ra, zero), jnp.where(beyond, rb, ra), jnp.where(beyond, zero, rb))
                    for b in range(3):
                        grid[c, block + b, pl.ds(row0 + rows, CHUNK), :] += placed[b]
        return carry

    listed = counts[lax.axis_index("ty"), lax.axis_index("tx")]
    lax.fori_loop(0, listed, slot_step, 0)

    grad_mid[...] = grid[:, :, margin : margin + length, :]
    for c in range(2):
        for b in range(4):
            at = slice((c * 4 + b) * margin, (c * 4 + b + 1) * margin)
            core_out[at, :] = grid[c, b, pl.ds(near, margin), :]
            chip_out[at, :] = grid[c, b, pl.ds(far, margin), :]
    kept, rows, _ = probe_keep.shape
    code = own_code(digit_groups())
    first_sent = core_out.shape[0] - kept * rows

    def place_piece(place, carry):
        piece = place ^ code
        probe_keep[place] = sums[pl.ds(pl.multiple_of(piece * rows, rows), rows), :]
        piece = (place + kept) ^ code
        core_out[pl.ds(pl.multiple_of(first_sent + place * rows, rows), rows), :] = sums[
            pl.ds(pl.multiple_of(piece * rows, rows), rows), :
        ]
        return carry

    lax.fori_loop(0, kept, place_piece, 0)


def rows_kernel(grad_mid, core_in, chip_in, to_left, to_right, inner):
    half = LANES
    odd = lax.axis_index("ty") % 2
    for c in range(2):
        for b in range(4):
            at = slice((c * 4 + b) * half, (c * 4 + b + 1) * half)
            core, chip = core_in[at, :], chip_in[at, :]
            for part in range(2):
                rows = slice(part * half, (part + 1) * half)
                value = grad_mid[c, b, rows, :] + jnp.where(odd == 1 - part, core, chip)
                if b == 0:
                    to_left[c, rows, :] = value
                elif b == 3:
                    to_right[c, rows, :] = value
                else:
                    inner[c, rows, (b - 1) * half : b * half] = value


def join_kernel(own, other, out):
    kept, rows, _ = own.shape
    _, modes, length, _ = out.shape
    code = own_code(digit_groups())
    each = length // rows

    for first, source in ((0, own), (kept, other)):

        def place_piece(place, carry, first=first, source=source):
            piece = (place + first) ^ code
            row = pl.multiple_of(piece % each * rows, rows)
            m = piece // each % modes
            c = piece // (each * modes) % 2
            b = pl.multiple_of(piece // (each * modes * 2) * LANES, LANES)
            out[c, m, pl.ds(row, rows), pl.ds(b, LANES)] = source[place]
            return carry

        lax.fori_loop(0, kept, place_piece, 0)


def shifted(value, axis, steps):
    count = lax.axis_size(axis)
    initial, last = (max(0, -steps), min(count, count - steps))
    return lax.ppermute(value, axis, [(source, source + steps) for source in range(initial, last)])


def exchanged(value, axis, mask):
    return lax.ppermute(value, axis, [(i, i ^ mask) for i in range(lax.axis_size(axis))])


def digit_groups():
    groups = [("ty", [1])]
    for axis, first in (("ty", 1), ("tx", 0)):
        bits = [1 << i for i in range(first, lax.axis_size(axis).bit_length() - 1)]
        groups += [(axis, bits[i : i + 2]) for i in range(0, len(bits), 2)]
    return groups


def masks(bits):
    return [sum(bit for i, bit in enumerate(reversed(bits)) if j >> i & 1) for j in range(1 << len(bits))]


def own_code(groups):
    code = 0
    for axis, bits in groups:
        index = lax.axis_index(axis)
        for bit in bits:
            code = code * 2 + (index // bit) % 2
    return code


def paired(value, mask_of):
    count = lax.axis_size("ty")
    pairs = [(i, i ^ 1) for i in range(count)] if mask_of == "core" else []
    if mask_of == "chip":
        for i in range(1, count - 1, 2):
            pairs += [(i, i + 1), (i + 1, i)]
    return lax.ppermute(value, "ty", pairs)


def reduce_step(value, axis, bits):
    places = masks(bits)
    count = value.shape[0] // len(places)
    taken = [exchanged(value[j * count : (j + 1) * count], axis, places[j]) for j in range(1, len(places))]
    return value[:count] + sum(taken[1:], taken[0])


def gather_step(value, axis, bits):
    return jnp.concatenate([value] + [exchanged(value, axis, mask) for mask in masks(bits)[1:]], axis=0)


def call(body, name, out, operands, scalars=0, scratch=(), limit=SMALL_LIMIT):
    vmem = pl.BlockSpec(memory_space=pltpu.VMEM)
    smem = pl.BlockSpec(memory_space=pltpu.SMEM)
    moved = sum(math.prod(v.shape) * v.dtype.itemsize for v in operands + tuple(out))
    return pl.pallas_call(
        body,
        out_shape=tuple(out),
        in_specs=[smem] * scalars + [vmem] * (len(operands) - scalars),
        out_specs=(vmem,) * len(out),
        scratch_shapes=list(scratch),
        compiler_params=pltpu.CompilerParams(vmem_limit_bytes=limit),
        cost_estimate=pl.CostEstimate(flops=0, bytes_accessed=moved, transcendentals=0),
        name=name,
    )(*operands)


def shards(object_field, probe_modes, intensities, offsets, counts):
    length = object_field.shape[1]
    modes, pattern = probe_modes.shape[1:3]
    margin = pattern // 2
    half = LANES
    devices = lax.axis_size("ty") * lax.axis_size("tx")
    groups = digit_groups()
    f32, bf16 = jnp.float32, jnp.bfloat16
    slots = intensities.shape[2]
    tables = jnp.asarray(fourier_tables(pattern))
    order = jnp.asarray(column_order(pattern))

    def shape(*sizes):
        return jax.ShapeDtypeStruct(sizes, f32)

    to_right, to_left, to_core, to_chip = call(
        edges_kernel, "edges", [shape(2, length, margin)] * 2 + [shape(2, margin, length)] * 2, (object_field,)
    )
    left = shifted(to_right, "tx", 1)
    right = shifted(to_left, "tx", -1)
    chip_rows = paired(to_chip, "chip")
    core_rows = paired(to_core, "core")
    (root,) = call(
        root_kernel,
        "root",
        [shape(slots, 2, half, pattern)],
        (intensities[0, 0], order),
        scratch=(pltpu.VMEM((slots, 2, pattern, half), f32),),
    )
    to_core, to_chip = call(corners_kernel, "corners", [shape(2, 2, margin, margin)] * 2, (left, right))
    chip_corners = paired(to_chip, "chip")
    core_corners = paired(to_core, "core")

    rows = 2 * 2 * modes * pattern // devices
    kept = devices // 2
    border = 2 * 4 * margin
    core_out, chip_out, grad_mid, probe_keep = call(
        slots_kernel,
        "slots",
        [shape(border + kept * rows, half), shape(border, half), shape(2, 4, length, half), shape(kept, rows, half)],
        (counts, offsets[0, 0], object_field, left, right, core_rows, chip_rows, core_corners, chip_corners, probe_modes, root, tables),
        scalars=2,
        scratch=(
            pltpu.VMEM((2, 4, length + 2 * margin, half), f32),
            pltpu.VMEM((2, 4, length + 2 * margin, half), f32),
            pltpu.VMEM((2, 2, pattern, half), f32),
            pltpu.VMEM((modes, 2, pattern, pattern), bf16),
            pltpu.VMEM((modes, 2, pattern, pattern), bf16),
            pltpu.VMEM((modes, 2, pattern, pattern), f32),
            pltpu.VMEM((2 * 2 * modes * pattern, half), f32),
        ),
        limit=VMEM_LIMIT,
    )

    core_in = paired(core_out, "core")
    chip_in = paired(chip_out, "chip")
    value = probe_keep + core_in[border:].reshape(probe_keep.shape)
    to_left, to_right, inner = call(
        rows_kernel, "rows", [shape(2, length, half)] * 2 + [shape(2, length, length)], (grad_mid, core_in[:border], chip_in)
    )
    from_right = shifted(to_left, "tx", -1)
    from_left = shifted(to_right, "tx", 1)
    inner = inner + jnp.concatenate([from_left, from_right], axis=2)

    for axis, bits in groups[1:]:
        value = reduce_step(value, axis, bits)
    value = value * (1.0 / devices)
    for axis, bits in reversed(groups[1:]):
        value = gather_step(value, axis, bits)
    other = paired(value, "core")
    (probe_grad,) = call(join_kernel, "join", [shape(*probe_modes.shape)], (value, other))
    return (inner, probe_grad)


def solution(mesh):
    placed = (
        P(None, "ty", "tx"),
        P(),
        P("ty", "tx", None, None, None),
        P("ty", "tx", None, None),
        P(),
    )
    return jax.shard_map(
        shards, mesh=mesh, in_specs=placed, out_specs=(P(None, "ty", "tx"), P()), check_vma=False
    )
```

```python
import functools
import math

import jax
import jax.numpy as jnp
import ml_dtypes
import numpy as np
from jax import lax
from jax.experimental import pallas as pl
from jax.experimental.pallas import tpu as pltpu
from jax.sharding import PartitionSpec as P

FLOOR = 0.5
LANES = 128
CHUNK = 32
VMEM_LIMIT = 28 * 1024 * 1024
MIDDLE_LIMIT = 12 * 1024 * 1024
SMALL_LIMIT = 8 * 1024 * 1024


def split_table(table):
    high = table.astype(ml_dtypes.bfloat16)
    low = (table - high.astype(np.float64)).astype(ml_dtypes.bfloat16)
    return high, low


def complex_block(matrix):
    return np.block([[matrix.real, matrix.imag], [-matrix.imag, matrix.real]])


@functools.lru_cache(maxsize=None)
def fourier_tables(pattern):
    half = pattern // 2
    n = np.arange(half)
    tables = []
    for parity in (0, 1):
        k = 2 * np.arange(half) + parity
        tables.append(np.exp(-2j * np.pi * ((n[:, None] * k[None, :]) % pattern) / pattern) / math.sqrt(pattern))
    forward = [complex_block(t) for t in tables]
    inverse = [complex_block(np.conj(t).T) for t in tables]
    every = forward + [t.T for t in forward] + [t.T for t in inverse] + inverse
    return np.stack([np.stack(split_table(t)) for t in every])


@functools.lru_cache(maxsize=None)
def column_order(pattern):
    return np.eye(pattern)[:, np.r_[0:pattern:2, 1:pattern:2]].astype(ml_dtypes.bfloat16)


def split(value):
    high = value.astype(jnp.bfloat16)
    low = (value - high.astype(jnp.float32)).astype(jnp.bfloat16)
    return high, low


def mul(a, b):
    return jnp.dot(a, b, preferred_element_type=jnp.float32)


def edges_kernel(center, kept, to_right, to_left, to_core, to_chip, core_right, core_left, chip_right, chip_left, sems):
    half = LANES
    odd = lax.axis_index("ty") % 2
    near = pl.ds(pl.multiple_of((1 - odd) * half, half), half)
    far = pl.ds(pl.multiple_of(odd * half, half), half)
    low, high = pl.ds(0, half), pl.ds(half, half)
    moves = (
        (center.at[:, :, high], to_right),
        (center.at[:, :, low], to_left),
        (center.at[:, near, :], to_core),
        (center.at[:, far, :], to_chip),
        (center.at[:, near, high], core_right),
        (center.at[:, near, low], core_left),
        (center.at[:, far, high], chip_right),
        (center.at[:, far, low], chip_left),
        (center, kept),
    )
    copies = [pltpu.make_async_copy(source, target, sems.at[i]) for i, (source, target) in enumerate(moves)]
    for copy in copies:
        copy.start()
    for copy in copies:
        copy.wait()


def prepare_kernel(measured, probe, order, root, probe_kept, held, halves, sems):
    first = pltpu.make_async_copy(measured, held, sems.at[0])
    second = pltpu.make_async_copy(probe, probe_kept, sems.at[1])
    first.start()
    second.start()
    first.wait()
    for slot in range(measured.shape[0]):
        for b in range(2):
            halves[slot, b] = jnp.sqrt(held[slot, :, b * LANES : (b + 1) * LANES])
        for parity in range(2):
            rows = pl.ds(parity, LANES, stride=2)
            high, low = split(jnp.concatenate([halves[slot, 0, rows, :], halves[slot, 1, rows, :]], axis=1))
            root[slot, parity] = mul(high, order[...]) + mul(low, order[...])
    second.wait()


def slots_kernel(
    counts, spots, center, left, right, core_rows, chip_rows,
    core_from_left, core_from_right, chip_from_left, chip_from_right, probe, root, tables,
    core_out, chip_out, grad_mid, probe_keep,
    pad, grid, patch, rows_high, rows_low, freq, sums,
):
    half = LANES
    modes = probe.shape[1]
    length = center.shape[1]
    margin = left.shape[2]
    odd = lax.axis_index("ty") % 2
    near = pl.multiple_of((1 - odd) * (margin + length), half)
    far = pl.multiple_of(odd * (margin + length), half)

    pad[:, 0, margin : margin + length, :] = left[...]
    pad[:, 3, margin : margin + length, :] = right[...]
    for b in range(2):
        cols = slice(b * half, (b + 1) * half)
        pad[:, 1 + b, margin : margin + length, :] = center[:, :, cols]
        pad[:, 1 + b, pl.ds(near, margin), :] = core_rows[:, :, cols]
        pad[:, 1 + b, pl.ds(far, margin), :] = chip_rows[:, :, cols]
    pad[:, 0, pl.ds(near, margin), :] = core_from_left[...]
    pad[:, 3, pl.ds(near, margin), :] = core_from_right[...]
    pad[:, 0, pl.ds(far, margin), :] = chip_from_left[...]
    pad[:, 3, pl.ds(far, margin), :] = chip_from_right[...]
    grid[...] = jnp.zeros_like(grid)
    sums[...] = jnp.zeros_like(sums)
    lane = lax.broadcasted_iota(jnp.int32, (CHUNK, half), 1)

    def slot_step(slot, carry):
        row0 = spots[0, slot]
        col0 = spots[1, slot]
        block = jnp.minimum(col0 // half, 1)
        shift = col0 - block * half
        back_shift = lax.rem(half - shift, half)
        fore_shift = lax.rem(shift, half)

        for chunk in range(half // CHUNK):
            spectra = []
            for part in range(2):
                rows = part * half + chunk * CHUNK
                here = slice(rows, rows + CHUNK)
                cells = []
                for c in range(2):
                    rolled = [
                        pltpu.roll(pad[c, block + b, pl.ds(row0 + rows, CHUNK), :], back_shift, 1) for b in range(3)
                    ]
                    for b in range(2):
                        cell = jnp.where(lane < half - shift, rolled[b], rolled[b + 1])
                        patch[c, b, here, :] = cell
                        cells.append(cell)
                lefts = []
                for m in range(modes):
                    waves = []
                    for b in range(2):
                        pr = probe[0, m, here, b * half : (b + 1) * half]
                        pi = probe[1, m, here, b * half : (b + 1) * half]
                        waves.append((pr * cells[b] - pi * cells[2 + b], pr * cells[2 + b] + pi * cells[b]))
                    (ra, ia), (rb, ib) = waves
                    lefts.append((jnp.concatenate([ra + rb, ia + ib], axis=1), jnp.concatenate([ra - rb, ia - ib], axis=1)))
                spectra.append(lefts)
            for parity in range(2):
                stacked = jnp.concatenate([spectra[part][m][parity] for m in range(modes) for part in range(2)], axis=0)
                high, low = split(stacked)
                out = mul(high, tables[parity, 0]) + (mul(low, tables[parity, 0]) + mul(high, tables[parity, 1]))
                for m in range(modes):
                    a = out[(2 * m) * CHUNK : (2 * m + 1) * CHUNK]
                    b = out[(2 * m + 1) * CHUNK : (2 * m + 2) * CHUNK]
                    for row_parity, value in enumerate((a + b, a - b)):
                        vh, vl = split(value)
                        for c in range(2):
                            at = slice(c * half + chunk * CHUNK, c * half + (chunk + 1) * CHUNK)
                            to = slice(parity * half, (parity + 1) * half)
                            rows_high[m, row_parity, at, to] = vh[:, c * half : (c + 1) * half]
                            rows_low[m, row_parity, at, to] = vl[:, c * half : (c + 1) * half]

        def row_transform(table):
            for m in range(modes):
                for parity in range(2):
                    high = rows_high[m, parity]
                    low = rows_low[m, parity]
                    freq[m, parity] = mul(tables[table + parity, 0], high) + (
                        mul(tables[table + parity, 1], high) + mul(tables[table + parity, 0], low)
                    )

        row_transform(2)

        for parity in range(2):
            for chunk in range(half // CHUNK):
                real = slice(chunk * CHUNK, (chunk + 1) * CHUNK)
                imag = slice(half + chunk * CHUNK, half + (chunk + 1) * CHUNK)
                values = [(freq[m, parity, real, :], freq[m, parity, imag, :]) for m in range(modes)]
                power = sum(re * re + im * im for re, im in values)
                factor = 1.0 - root[slot, parity, real, :] * lax.rsqrt(jnp.maximum(power, FLOOR * FLOOR))
                for m in range(modes):
                    for at, value in zip((real, imag), values[m]):
                        vh, vl = split(value * factor)
                        rows_high[m, parity, at, :] = vh
                        rows_low[m, parity, at, :] = vl

        row_transform(4)

        for chunk in range(half // CHUNK):
            real = slice(chunk * CHUNK, (chunk + 1) * CHUNK)
            imag = slice(half + chunk * CHUNK, half + (chunk + 1) * CHUNK)
            backs = []
            for q in range(2):
                cols = slice(q * half, (q + 1) * half)
                pieces = []
                for m in range(modes):
                    even = jnp.concatenate([freq[m, 0, real, cols], freq[m, 0, imag, cols]], axis=1)
                    odd = jnp.concatenate([freq[m, 1, real, cols], freq[m, 1, imag, cols]], axis=1)
                    pieces += [even + odd, even - odd]
                high, low = split(jnp.concatenate(pieces, axis=0))
                backs.append(mul(high, tables[6 + q, 0]) + (mul(low, tables[6 + q, 0]) + mul(high, tables[6 + q, 1])))
            halves = (backs[0] + backs[1], backs[0] - backs[1])
            for part in range(2):
                rows = part * half + chunk * CHUNK
                here = slice(rows, rows + CHUNK)
                total = [[0.0, 0.0], [0.0, 0.0]]
                for b in range(2):
                    xr = patch[0, b, here, :]
                    xi = patch[1, b, here, :]
                    for m in range(modes):
                        at = (2 * m + part) * CHUNK
                        br = halves[b][at : at + CHUNK, :half]
                        bi = halves[b][at : at + CHUNK, half:]
                        pr = probe[0, m, here, b * half : (b + 1) * half]
                        pi = probe[1, m, here, b * half : (b + 1) * half]
                        total[0][b] += pr * br + pi * bi
                        total[1][b] += pr * bi - pi * br
                        sums[pl.ds(((b * 2 + 0) * modes + m) * length + rows, CHUNK), :] += xr * br + xi * bi
                        sums[pl.ds(((b * 2 + 1) * modes + m) * length + rows, CHUNK), :] += xr * bi - xi * br
                for c in range(2):
                    ra = pltpu.roll(total[c][0], fore_shift, 1)
                    rb = pltpu.roll(total[c][1], fore_shift, 1)
                    beyond = lane >= shift
                    zero = jnp.zeros_like(ra)
                    placed = (jnp.where(beyond, ra, zero), jnp.where(beyond, rb, ra), jnp.where(beyond, zero, rb))
                    for b in range(3):
                        grid[c, block + b, pl.ds(row0 + rows, CHUNK), :] += placed[b]
        return carry

    listed = counts[lax.axis_index("tx"), lax.axis_index("ty")]
    lax.fori_loop(0, listed, slot_step, 0)

    grad_mid[...] = grid[:, :, margin : margin + length, :]
    for c in range(2):
        for b in range(4):
            at = slice((c * 4 + b) * margin, (c * 4 + b + 1) * margin)
            core_out[at, :] = grid[c, b, pl.ds(near, margin), :]
            chip_out[at, :] = grid[c, b, pl.ds(far, margin), :]
    kept, rows, _ = probe_keep.shape
    code = own_code(digit_groups())
    first_sent = core_out.shape[0] - kept * rows

    def place_piece(place, carry):
        piece = place ^ code
        probe_keep[place] = sums[pl.ds(pl.multiple_of(piece * rows, rows), rows), :]
        piece = (place + kept) ^ code
        core_out[pl.ds(pl.multiple_of(first_sent + place * rows, rows), rows), :] = sums[
            pl.ds(pl.multiple_of(piece * rows, rows), rows), :
        ]
        return carry

    lax.fori_loop(0, kept, place_piece, 0)


def rows_kernel(grad_mid, core_in, chip_in, own, one, two, three, to_left, to_right, inner, joined):
    half = LANES
    odd = lax.axis_index("ty") % 2
    for c in range(2):
        for b in range(4):
            at = slice((c * 4 + b) * half, (c * 4 + b + 1) * half)
            core, chip = core_in[at, :], chip_in[at, :]
            for part in range(2):
                rows = slice(part * half, (part + 1) * half)
                value = grad_mid[c, b, rows, :] + jnp.where(odd == 1 - part, core, chip)
                if b == 0:
                    to_left[c, rows, :] = value
                elif b == 3:
                    to_right[c, rows, :] = value
                else:
                    inner[c, rows, (b - 1) * half : b * half] = value
    join_pieces((own, one, two, three), joined)


def columns_kernel(inner, from_left, from_right, own, one, two, three, grad, joined):
    half = LANES
    grad[:, :, :half] = inner[:, :, :half] + from_left[...]
    grad[:, :, half:] = inner[:, :, half:] + from_right[...]
    join_pieces((own, one, two, three), joined)


def join_pieces(pieces, joined):
    count = pieces[0].shape[0]
    for i, piece in enumerate(pieces):
        joined[i * count : (i + 1) * count] = piece[...]


def join_kernel(own, other, out):
    kept, rows, _ = own.shape
    _, modes, length, _ = out.shape
    code = own_code(digit_groups())
    each = length // rows

    for first, source in ((0, own), (kept, other)):

        def place_piece(place, carry, first=first, source=source):
            piece = (place + first) ^ code
            row = pl.multiple_of(piece % each * rows, rows)
            m = piece // each % modes
            c = piece // (each * modes) % 2
            b = pl.multiple_of(piece // (each * modes * 2) * LANES, LANES)
            out[c, m, pl.ds(row, rows), pl.ds(b, LANES)] = source[place]
            return carry

        lax.fori_loop(0, kept, place_piece, 0)


def shifted(value, axis, steps):
    count = lax.axis_size(axis)
    initial, last = (max(0, -steps), min(count, count - steps))
    return lax.ppermute(value, axis, [(source, source + steps) for source in range(initial, last)])


def exchanged(value, axis, mask):
    return lax.ppermute(value, axis, [(i, i ^ mask) for i in range(lax.axis_size(axis))])


def digit_groups():
    groups = [("ty", [1])]
    for axis, first in (("ty", 1), ("tx", 0)):
        bits = [1 << i for i in range(first, lax.axis_size(axis).bit_length() - 1)]
        groups += [(axis, bits[i : i + 2]) for i in range(0, len(bits), 2)]
    return groups


def masks(bits):
    return [sum(bit for i, bit in enumerate(reversed(bits)) if j >> i & 1) for j in range(1 << len(bits))]


def own_code(groups):
    code = 0
    for axis, bits in groups:
        index = lax.axis_index(axis)
        for bit in bits:
            code = code * 2 + (index // bit) % 2
    return code


def paired(value, mask_of):
    count = lax.axis_size("ty")
    pairs = [(i, i ^ 1) for i in range(count)] if mask_of == "core" else []
    if mask_of == "chip":
        for i in range(1, count - 1, 2):
            pairs += [(i, i + 1), (i + 1, i)]
    return lax.ppermute(value, "ty", pairs)


def cornered(value, mask_of, steps):
    rows, cols = lax.axis_size("ty"), lax.axis_size("tx")
    pairs = []
    for a in range(rows):
        other = a ^ 1 if mask_of == "core" else a + 1 if a % 2 else a - 1
        for b in range(cols):
            if 0 <= other < rows and 0 <= b + steps < cols:
                pairs.append((a * cols + b, other * cols + b + steps))
    return lax.ppermute(value, ("ty", "tx"), pairs)


def reduce_step(value, axis, bits):
    places = masks(bits)
    count = value.shape[0] // len(places)
    taken = [exchanged(value[j * count : (j + 1) * count], axis, places[j]) for j in range(1, len(places))]
    return value[:count] + sum(taken[1:], taken[0])


def gathered(value, axis, bits):
    return [value] + [exchanged(value, axis, mask) for mask in masks(bits)[1:]]


def call(body, name, out, operands, spaces="", scratch=(), limit=SMALL_LIMIT):
    kinds = {"v": pltpu.VMEM, "s": pltpu.SMEM, "a": pl.ANY}
    spaces = spaces + "v" * (len(operands) - len(spaces))
    moved = sum(math.prod(v.shape) * v.dtype.itemsize for v in tuple(operands) + tuple(out))
    return pl.pallas_call(
        body,
        out_shape=tuple(out),
        in_specs=[pl.BlockSpec(memory_space=kinds[space]) for space in spaces],
        out_specs=(pl.BlockSpec(memory_space=pltpu.VMEM),) * len(out),
        scratch_shapes=list(scratch),
        compiler_params=pltpu.CompilerParams(vmem_limit_bytes=limit),
        cost_estimate=pl.CostEstimate(flops=0, bytes_accessed=moved, transcendentals=0),
        name=name,
    )(*operands)


def shards(object_field, probe_modes, intensities, offsets, counts):
    length = object_field.shape[1]
    modes, pattern = probe_modes.shape[1:3]
    margin = pattern // 2
    half = LANES
    devices = lax.axis_size("ty") * lax.axis_size("tx")
    groups = digit_groups()
    f32, bf16 = jnp.float32, jnp.bfloat16
    slots = intensities.shape[2]
    tables = jnp.asarray(fourier_tables(pattern))
    order = jnp.asarray(column_order(pattern))

    def shape(*sizes):
        return jax.ShapeDtypeStruct(sizes, f32)

    center, to_right, to_left, to_core, to_chip, core_right, core_left, chip_right, chip_left = call(
        edges_kernel,
        "edges",
        [shape(2, length, length)] + [shape(2, length, margin)] * 2 + [shape(2, margin, length)] * 2 + [shape(2, margin, margin)] * 4,
        (object_field,),
        "a",
        scratch=(pltpu.SemaphoreType.DMA((9,)),),
    )
    left = shifted(to_right, "tx", 1)
    right = shifted(to_left, "tx", -1)
    core_rows = paired(to_core, "core")
    chip_rows = paired(to_chip, "chip")
    corners = [
        cornered(core_right, "core", 1),
        cornered(core_left, "core", -1),
        cornered(chip_right, "chip", 1),
        cornered(chip_left, "chip", -1),
    ]
    root, probe = call(
        prepare_kernel,
        "prepare",
        [shape(slots, 2, half, pattern), shape(*probe_modes.shape)],
        (intensities[0, 0], probe_modes, order),
        "aa",
        scratch=(
            pltpu.VMEM((slots, pattern, pattern), f32),
            pltpu.VMEM((slots, 2, pattern, half), f32),
            pltpu.SemaphoreType.DMA((2,)),
        ),
        limit=MIDDLE_LIMIT,
    )

    rows = 2 * 2 * modes * pattern // devices
    kept = devices // 2
    border = 2 * 4 * margin
    core_out, chip_out, grad_mid, probe_keep = call(
        slots_kernel,
        "slots",
        [shape(border + kept * rows, half), shape(border, half), shape(2, 4, length, half), shape(kept, rows, half)],
        (counts.T, offsets[0, 0].T, center, left, right, core_rows, chip_rows, *corners, probe, root, tables),
        "ss",
        scratch=(
            pltpu.VMEM((2, 4, length + 2 * margin, half), f32),
            pltpu.VMEM((2, 4, length + 2 * margin, half), f32),
            pltpu.VMEM((2, 2, pattern, half), f32),
            pltpu.VMEM((modes, 2, pattern, pattern), bf16),
            pltpu.VMEM((modes, 2, pattern, pattern), bf16),
            pltpu.VMEM((modes, 2, pattern, pattern), f32),
            pltpu.VMEM((2 * 2 * modes * pattern, half), f32),
        ),
        limit=VMEM_LIMIT,
    )

    core_in = paired(core_out, "core")
    chip_in = paired(chip_out, "chip")
    value = probe_keep + core_in[border:].reshape(probe_keep.shape)
    for axis, bits in groups[1:]:
        value = reduce_step(value, axis, bits)
    value = value * (1.0 / devices)
    last = len(groups) - 1
    for i in range(last, 0, -1):
        pieces = gathered(value, *groups[i])
        joined = shape(len(pieces) * value.shape[0], rows, half)
        if i == last:
            assert len(pieces) == 4
            to_left, to_right, inner, value = call(
                rows_kernel,
                "rows",
                [shape(2, length, half)] * 2 + [shape(2, length, length), joined],
                (grad_mid, core_in[:border], chip_in, *pieces),
            )
            from_right = shifted(to_left, "tx", -1)
            from_left = shifted(to_right, "tx", 1)
        elif i == 1 and len(pieces) == 4:
            inner, value = call(
                columns_kernel, "columns", [shape(2, length, length), joined], (inner, from_left, from_right, *pieces)
            )
        else:
            value = jnp.concatenate(pieces, axis=0)
    if len(groups) < 3 or len(groups[1][1]) != 2:
        inner = inner + jnp.concatenate([from_left, from_right], axis=2)
    other = paired(value, "core")
    (probe_grad,) = call(join_kernel, "join", [shape(*probe_modes.shape)], (value, other))
    return (inner, probe_grad)


def solution(mesh):
    placed = (
        P(None, "ty", "tx"),
        P(),
        P("ty", "tx", None, None, None),
        P("ty", "tx", None, None),
        P(),
    )
    return jax.shard_map(
        shards, mesh=mesh, in_specs=placed, out_specs=(P(None, "ty", "tx"), P()), check_vma=False
    )
```

```python
import functools
import math

import jax
import jax.numpy as jnp
import ml_dtypes
import numpy as np
from jax import lax
from jax.experimental import pallas as pl
from jax.experimental.pallas import tpu as pltpu
from jax.sharding import PartitionSpec as P

FLOOR = 0.5
LANES = 128
CHUNK = 32
HEAVY = 200_000_000
VMEM_LIMIT = 28 * 1024 * 1024
MIDDLE_LIMIT = 12 * 1024 * 1024
SMALL_LIMIT = 8 * 1024 * 1024


def split_table(table):
    high = table.astype(ml_dtypes.bfloat16)
    low = (table - high.astype(np.float64)).astype(ml_dtypes.bfloat16)
    return high, low


def complex_block(matrix):
    return np.block([[matrix.real, matrix.imag], [-matrix.imag, matrix.real]])


@functools.lru_cache(maxsize=None)
def fourier_tables(pattern):
    half = pattern // 2
    n = np.arange(half)
    tables = []
    for parity in (0, 1):
        k = 2 * np.arange(half) + parity
        tables.append(np.exp(-2j * np.pi * ((n[:, None] * k[None, :]) % pattern) / pattern) / math.sqrt(pattern))
    forward = [complex_block(t) for t in tables]
    inverse = [complex_block(np.conj(t).T) for t in tables]
    every = forward + [t.T for t in forward] + [t.T for t in inverse] + inverse
    return np.stack([np.stack(split_table(t)) for t in every])


@functools.lru_cache(maxsize=None)
def column_order(pattern):
    return np.eye(pattern)[:, np.r_[0:pattern:2, 1:pattern:2]].astype(ml_dtypes.bfloat16)


def split(value):
    high = value.astype(jnp.bfloat16)
    low = (value - high.astype(jnp.float32)).astype(jnp.bfloat16)
    return high, low


def mul(a, b):
    return jnp.dot(a, b, preferred_element_type=jnp.float32)


def near_and_far(unit):
    odd = lax.axis_index("ty") % 2
    return pl.multiple_of((1 - odd) * unit, LANES), pl.multiple_of(odd * unit, LANES)


def inner_and_outer():
    odd = lax.axis_index("tx") % 2
    return pl.multiple_of((1 - odd) * LANES, LANES), pl.multiple_of(odd * LANES, LANES)


def edges_kernel(field, center, core_rows, chip_rows, inner_corner, outer_corner, sems):
    half = LANES
    near, far = (pl.ds(start, half) for start in near_and_far(half))
    inner, outer = (pl.ds(start, half) for start in inner_and_outer())
    moves = (
        (field.at[:, near, :], core_rows),
        (field.at[:, far, inner], inner_corner),
        (field.at[:, far, outer], outer_corner),
        (field.at[:, far, :], chip_rows),
        (field, center),
    )
    copies = [pltpu.make_async_copy(source, target, sems.at[i]) for i, (source, target) in enumerate(moves)]
    for copy in copies:
        copy.start()
    for copy in copies:
        copy.wait()


def sides_kernel(center, core_rows, inner_side, outer_side):
    half = LANES
    length = center.shape[1]
    odd = lax.axis_index("ty") % 2
    own, other = pl.multiple_of(odd * half, half), pl.multiple_of((1 - odd) * length, half)
    for target, start in zip((inner_side, outer_side), inner_and_outer()):
        cols = pl.ds(start, half)
        target[:, pl.ds(own, length), :] = center[:, :, cols]
        target[:, pl.ds(other, half), :] = core_rows[:, :, cols]


def prepare_kernel(counts, spots, order, measured, probe, root, probe_kept, scalars, held, halves, sems):
    first = pltpu.make_async_copy(measured, held, sems.at[0])
    second = pltpu.make_async_copy(probe, probe_kept, sems.at[1])
    first.start()
    second.start()
    scalars[0] = counts[lax.axis_index("tx"), lax.axis_index("ty")]
    for slot in range(spots.shape[1]):
        for axis in range(2):
            scalars[1 + 2 * slot + axis] = spots[axis, slot]
    first.wait()
    for slot in range(measured.shape[0]):
        for b in range(2):
            halves[slot, b] = jnp.sqrt(held[slot, :, b * LANES : (b + 1) * LANES])
        for parity in range(2):
            rows = pl.ds(parity, LANES, stride=2)
            high, low = split(jnp.concatenate([halves[slot, 0, rows, :], halves[slot, 1, rows, :]], axis=1))
            root[slot, parity] = mul(high, order[...]) + mul(low, order[...])
    second.wait()


def slots_kernel(
    scalars, center, core_rows, chip_rows, inner_side, outer_side, inner_corner, outer_corner, probe, root, tables,
    probe_sent, probe_keep, inner_side_out, outer_side_out, inner_corner_out, outer_corner_out, chip_out, grad_mid,
    pad, grid, patch, rows_high, rows_low, freq, sums,
):
    half = LANES
    modes = probe.shape[1]
    length = center.shape[1]
    margin = core_rows.shape[1]
    tall = inner_side.shape[1]
    near, far = near_and_far(margin + length)
    long_start = pl.multiple_of((1 - lax.axis_index("ty") % 2) * margin, half)
    near, far, both = pl.ds(near, margin), pl.ds(far, margin), pl.ds(long_start, tall)
    inner = (1 - lax.axis_index("tx") % 2) * 3
    outer = 3 - inner

    for b in range(2):
        cols = slice(b * half, (b + 1) * half)
        pad[:, 1 + b, margin : margin + length, :] = center[:, :, cols]
        pad[:, 1 + b, near, :] = core_rows[:, :, cols]
        pad[:, 1 + b, far, :] = chip_rows[:, :, cols]
    pad[:, inner, both, :] = inner_side[...]
    pad[:, outer, both, :] = outer_side[...]
    pad[:, inner, far, :] = inner_corner[...]
    pad[:, outer, far, :] = outer_corner[...]
    grid[...] = jnp.zeros_like(grid)
    sums[...] = jnp.zeros_like(sums)
    lane = lax.broadcasted_iota(jnp.int32, (CHUNK, half), 1)

    def slot_step(slot, carry):
        row0 = scalars[1 + 2 * slot]
        col0 = scalars[2 + 2 * slot]
        block = jnp.minimum(col0 // half, 1)
        shift = col0 - block * half
        back_shift = lax.rem(half - shift, half)
        fore_shift = lax.rem(shift, half)

        for chunk in range(half // CHUNK):
            spectra = []
            for part in range(2):
                rows = part * half + chunk * CHUNK
                here = slice(rows, rows + CHUNK)
                cells = []
                for c in range(2):
                    rolled = [
                        pltpu.roll(pad[c, block + b, pl.ds(row0 + rows, CHUNK), :], back_shift, 1) for b in range(3)
                    ]
                    for b in range(2):
                        cell = jnp.where(lane < half - shift, rolled[b], rolled[b + 1])
                        patch[c, b, here, :] = cell
                        cells.append(cell)
                lefts = []
                for m in range(modes):
                    waves = []
                    for b in range(2):
                        pr = probe[0, m, here, b * half : (b + 1) * half]
                        pi = probe[1, m, here, b * half : (b + 1) * half]
                        waves.append((pr * cells[b] - pi * cells[2 + b], pr * cells[2 + b] + pi * cells[b]))
                    (ra, ia), (rb, ib) = waves
                    lefts.append((jnp.concatenate([ra + rb, ia + ib], axis=1), jnp.concatenate([ra - rb, ia - ib], axis=1)))
                spectra.append(lefts)
            for parity in range(2):
                stacked = jnp.concatenate([spectra[part][m][parity] for m in range(modes) for part in range(2)], axis=0)
                high, low = split(stacked)
                out = mul(high, tables[parity, 0]) + (mul(low, tables[parity, 0]) + mul(high, tables[parity, 1]))
                for m in range(modes):
                    a = out[(2 * m) * CHUNK : (2 * m + 1) * CHUNK]
                    b = out[(2 * m + 1) * CHUNK : (2 * m + 2) * CHUNK]
                    for row_parity, value in enumerate((a + b, a - b)):
                        vh, vl = split(value)
                        for c in range(2):
                            at = slice(c * half + chunk * CHUNK, c * half + (chunk + 1) * CHUNK)
                            to = slice(parity * half, (parity + 1) * half)
                            rows_high[m, row_parity, at, to] = vh[:, c * half : (c + 1) * half]
                            rows_low[m, row_parity, at, to] = vl[:, c * half : (c + 1) * half]

        def row_transform(table):
            for m in range(modes):
                for parity in range(2):
                    high = rows_high[m, parity]
                    low = rows_low[m, parity]
                    freq[m, parity] = mul(tables[table + parity, 0], high) + (
                        mul(tables[table + parity, 1], high) + mul(tables[table + parity, 0], low)
                    )

        row_transform(2)

        for parity in range(2):
            for chunk in range(half // CHUNK):
                real = slice(chunk * CHUNK, (chunk + 1) * CHUNK)
                imag = slice(half + chunk * CHUNK, half + (chunk + 1) * CHUNK)
                values = [(freq[m, parity, real, :], freq[m, parity, imag, :]) for m in range(modes)]
                power = sum(re * re + im * im for re, im in values)
                factor = 1.0 - root[slot, parity, real, :] * lax.rsqrt(jnp.maximum(power, FLOOR * FLOOR))
                for m in range(modes):
                    for at, value in zip((real, imag), values[m]):
                        vh, vl = split(value * factor)
                        rows_high[m, parity, at, :] = vh
                        rows_low[m, parity, at, :] = vl

        row_transform(4)

        for chunk in range(half // CHUNK):
            real = slice(chunk * CHUNK, (chunk + 1) * CHUNK)
            imag = slice(half + chunk * CHUNK, half + (chunk + 1) * CHUNK)
            backs = []
            for q in range(2):
                cols = slice(q * half, (q + 1) * half)
                pieces = []
                for m in range(modes):
                    even = jnp.concatenate([freq[m, 0, real, cols], freq[m, 0, imag, cols]], axis=1)
                    odd = jnp.concatenate([freq[m, 1, real, cols], freq[m, 1, imag, cols]], axis=1)
                    pieces += [even + odd, even - odd]
                high, low = split(jnp.concatenate(pieces, axis=0))
                backs.append(mul(high, tables[6 + q, 0]) + (mul(low, tables[6 + q, 0]) + mul(high, tables[6 + q, 1])))
            halves = (backs[0] + backs[1], backs[0] - backs[1])
            for part in range(2):
                rows = part * half + chunk * CHUNK
                here = slice(rows, rows + CHUNK)
                total = [[0.0, 0.0], [0.0, 0.0]]
                for b in range(2):
                    xr = patch[0, b, here, :]
                    xi = patch[1, b, here, :]
                    for m in range(modes):
                        at = (2 * m + part) * CHUNK
                        br = halves[b][at : at + CHUNK, :half]
                        bi = halves[b][at : at + CHUNK, half:]
                        pr = probe[0, m, here, b * half : (b + 1) * half]
                        pi = probe[1, m, here, b * half : (b + 1) * half]
                        total[0][b] += pr * br + pi * bi
                        total[1][b] += pr * bi - pi * br
                        sums[pl.ds(((b * 2 + 0) * modes + m) * length + rows, CHUNK), :] += xr * br + xi * bi
                        sums[pl.ds(((b * 2 + 1) * modes + m) * length + rows, CHUNK), :] += xr * bi - xi * br
                for c in range(2):
                    ra = pltpu.roll(total[c][0], fore_shift, 1)
                    rb = pltpu.roll(total[c][1], fore_shift, 1)
                    beyond = lane >= shift
                    zero = jnp.zeros_like(ra)
                    placed = (jnp.where(beyond, ra, zero), jnp.where(beyond, rb, ra), jnp.where(beyond, zero, rb))
                    for b in range(3):
                        grid[c, block + b, pl.ds(row0 + rows, CHUNK), :] += placed[b]
        return carry

    lax.fori_loop(0, scalars[0], slot_step, 0)

    kept, rows, _ = probe_keep.shape
    code = own_code(digit_groups())

    def place_piece(place, carry):
        for first, target in ((0, probe_keep), (kept, probe_sent)):
            piece = (place + first) ^ code
            target[place] = sums[pl.ds(pl.multiple_of(piece * rows, rows), rows), :]
        return carry

    lax.fori_loop(0, kept, place_piece, 0)
    inner_side_out[...] = grid[:, inner, both, :]
    outer_side_out[...] = grid[:, outer, both, :]
    inner_corner_out[...] = grid[:, inner, far, :]
    outer_corner_out[...] = grid[:, outer, far, :]
    for b in range(2):
        cols = slice(b * half, (b + 1) * half)
        chip_out[:, :, cols] = grid[:, 1 + b, far, :]
        grad_mid[:, :, cols] = grid[:, 1 + b, both, :]


def rows_kernel(grad_mid, inner_side, outer_side, chip_in, inner_corner, outer_corner, own, other, core_out, inner_grad, joined):
    half = LANES
    length = inner_grad.shape[1]
    odd = lax.axis_index("ty") % 2
    near_rows = pl.ds(pl.multiple_of((1 - odd) * length, half), half)
    near, far = (pl.ds(start, half) for start in near_and_far(half))
    near_own = pl.ds(pl.multiple_of(half, half), half)
    far_own = pl.ds(pl.multiple_of(odd * length, half), half)
    for side, corner, start in zip((inner_side, outer_side), (inner_corner, outer_corner), inner_and_outer()):
        cols = pl.ds(start, half)
        core_out[:, :, cols] = grad_mid[:, near_rows, cols] + side[:, near_rows, :]
        inner_grad[:, near, cols] = grad_mid[:, near_own, cols] + side[:, near_own, :]
        inner_grad[:, far, cols] = (grad_mid[:, far_own, cols] + side[:, far_own, :]) + (chip_in[:, :, cols] + corner[...])
    join_pieces((own, other), joined)


def columns_kernel(inner_grad, core_in, *refs):
    pieces, (grad, joined) = refs[:-2], refs[-2:]
    near, far = (pl.ds(start, LANES) for start in near_and_far(LANES))
    grad[:, near, :] = inner_grad[:, near, :] + core_in[...]
    grad[:, far, :] = inner_grad[:, far, :]
    join_pieces(pieces, joined)


def join_pieces(pieces, joined):
    count = pieces[0].shape[0]
    for i, piece in enumerate(pieces):
        joined[i * count : (i + 1) * count] = piece[...]


def join_kernel(own, other, out):
    kept, rows, _ = own.shape
    _, modes, length, _ = out.shape
    code = own_code(digit_groups())
    each = length // rows

    for first, source in ((0, own), (kept, other)):

        def place_piece(place, carry, first=first, source=source):
            piece = (place + first) ^ code
            row = pl.multiple_of(piece % each * rows, rows)
            m = piece // each % modes
            c = piece // (each * modes) % 2
            b = pl.multiple_of(piece // (each * modes * 2) * LANES, LANES)
            out[c, m, pl.ds(row, rows), pl.ds(b, LANES)] = source[place]
            return carry

        lax.fori_loop(0, kept, place_piece, 0)


def exchanged(value, axis, mask):
    return lax.ppermute(value, axis, [(i, i ^ mask) for i in range(lax.axis_size(axis))])


def digit_groups():
    groups = [("ty", [1])]
    bits = [1 << i for i in range(1, lax.axis_size("ty").bit_length() - 1)]
    groups += [("ty", bits[i : i + 2]) for i in range(0, len(bits), 2)]
    return groups + [("tx", [1])]


def masks(bits):
    return [sum(bit for i, bit in enumerate(reversed(bits)) if j >> i & 1) for j in range(1 << len(bits))]


def own_code(groups):
    code = 0
    for axis, bits in groups:
        index = lax.axis_index(axis)
        for bit in bits:
            code = code * 2 + (index // bit) % 2
    return code


def pair_partner(index, kind):
    return index ^ 1 if kind == "inner" else index + 1 if index % 2 else index - 1


def paired(value, axis, kind):
    count = lax.axis_size(axis)
    pairs = [(i, pair_partner(i, kind)) for i in range(count)]
    return lax.ppermute(value, axis, [(i, j) for i, j in pairs if 0 <= j < count])


def cornered(value, kind):
    rows, cols = lax.axis_size("ty"), lax.axis_size("tx")
    pairs = []
    for a in range(rows):
        for b in range(cols):
            i, j = pair_partner(a, "outer"), pair_partner(b, kind)
            if 0 <= i < rows and 0 <= j < cols:
                pairs.append((a * cols + b, i * cols + j))
    return lax.ppermute(value, ("ty", "tx"), pairs)


def add_kernel(scale, own, *refs):
    others, out = refs[:-1], refs[-1]
    count = out.shape[0]
    total = own[:count]
    for other in others:
        total += other[...]
    out[...] = total * scale


def added(own, others, scale=1.0, weight=0):
    out = jax.ShapeDtypeStruct(others[0].shape, jnp.float32)
    (result,) = call(functools.partial(add_kernel, scale), "add", [out], (own, *others), weight=weight)
    return result


def reduce_step(value, axis, bits, scale=1.0, weight=0):
    places = masks(bits)
    count = value.shape[0] // len(places)
    taken = [exchanged(value[j * count : (j + 1) * count], axis, places[j]) for j in range(1, len(places))]
    return added(value, taken, scale, weight)


def gathered(value, axis, bits):
    return [value] + [exchanged(value, axis, mask) for mask in masks(bits)[1:]]


def call(body, name, out, operands, spaces="", results="", scratch=(), limit=SMALL_LIMIT, weight=0):
    kinds = {"v": pltpu.VMEM, "s": pltpu.SMEM, "h": pltpu.HBM}

    def specs(letters, count):
        return tuple(pl.BlockSpec(memory_space=kinds[x]) for x in letters + "v" * (count - len(letters)))

    moved = weight + sum(math.prod(v.shape) * v.dtype.itemsize for v in tuple(operands) + tuple(out))
    return pl.pallas_call(
        body,
        out_shape=tuple(out),
        in_specs=specs(spaces, len(operands)),
        out_specs=specs(results, len(out)),
        scratch_shapes=list(scratch),
        compiler_params=pltpu.CompilerParams(vmem_limit_bytes=limit),
        cost_estimate=pl.CostEstimate(flops=0, bytes_accessed=moved, transcendentals=0),
        name=name,
    )(*operands)


def shards(object_field, probe_modes, intensities, offsets, counts):
    length = object_field.shape[1]
    modes, pattern = probe_modes.shape[1:3]
    margin = pattern // 2
    half = LANES
    devices = lax.axis_size("ty") * lax.axis_size("tx")
    groups = digit_groups()
    f32, bf16 = jnp.float32, jnp.bfloat16
    slots = intensities.shape[2]
    tables = jnp.asarray(fourier_tables(pattern))
    order = jnp.asarray(column_order(pattern))

    def shape(*sizes):
        return jax.ShapeDtypeStruct(sizes, f32)

    tile, rows_shape, side, corner = shape(2, length, length), shape(2, margin, length), shape(2, length + margin, margin), shape(2, margin, margin)
    center, core_rows, chip_rows, inner_corner, outer_corner = call(
        edges_kernel,
        "edges",
        [tile, rows_shape, rows_shape, corner, corner],
        (object_field,),
        "h",
        scratch=(pltpu.SemaphoreType.DMA((5,)),),
    )
    core_rows = paired(core_rows, "ty", "inner")
    inner_corner = cornered(inner_corner, "inner")
    outer_corner = cornered(outer_corner, "outer")
    chip_rows = paired(chip_rows, "ty", "outer")
    inner_side, outer_side = call(sides_kernel, "sides", [side, side], (center, core_rows), weight=HEAVY)
    inner_side = paired(inner_side, "tx", "inner")
    outer_side = paired(outer_side, "tx", "outer")
    root, probe, scalars = call(
        prepare_kernel,
        "prepare",
        [shape(slots, 2, half, pattern), shape(*probe_modes.shape), jax.ShapeDtypeStruct((1 + 2 * slots,), jnp.int32)],
        (counts.T, offsets[0, 0].T, order, intensities[0, 0], probe_modes),
        "ssvhh",
        "vvs",
        scratch=(
            pltpu.VMEM((slots, pattern, pattern), f32),
            pltpu.VMEM((slots, 2, pattern, half), f32),
            pltpu.SemaphoreType.DMA((2,)),
        ),
        limit=MIDDLE_LIMIT,
    )

    pieces = 1 << sum(len(bits) for _, bits in groups)
    rows = 2 * 2 * modes * pattern // pieces
    kept = shape(pieces // 2, rows, half)
    probe_sent, value, inner_side, outer_side, inner_corner, outer_corner, chip_rows, grad_mid = call(
        slots_kernel,
        "slots",
        [kept, kept, side, side, corner, corner, rows_shape, shape(2, length + margin, length)],
        (scalars, center, core_rows, chip_rows, inner_side, outer_side, inner_corner, outer_corner, probe, root, tables),
        "s",
        scratch=(
            pltpu.VMEM((2, 4, length + 2 * margin, half), f32),
            pltpu.VMEM((2, 4, length + 2 * margin, half), f32),
            pltpu.VMEM((2, 2, pattern, half), f32),
            pltpu.VMEM((modes, 2, pattern, pattern), bf16),
            pltpu.VMEM((modes, 2, pattern, pattern), bf16),
            pltpu.VMEM((modes, 2, pattern, pattern), f32),
            pltpu.VMEM((2 * 2 * modes * pattern, half), f32),
        ),
        limit=VMEM_LIMIT,
    )

    value = added(value, [paired(probe_sent, "ty", "inner")], weight=HEAVY)
    inner_side = paired(inner_side, "tx", "inner")
    outer_side = paired(outer_side, "tx", "outer")
    for axis, bits in groups[1:-1]:
        value = reduce_step(value, axis, bits)
    value = reduce_step(value, *groups[-1], scale=1.0 / devices, weight=HEAVY)
    for i in range(1, lax.axis_size("tx").bit_length() - 1):
        value = added(value, [exchanged(value, "tx", 1 << i)])
    chip_rows = paired(chip_rows, "ty", "outer")
    inner_corner = cornered(inner_corner, "inner")
    outer_corner = cornered(outer_corner, "outer")
    for i in range(len(groups) - 1, 0, -1):
        parts = gathered(value, *groups[i])
        joined = shape(len(parts) * value.shape[0], rows, half)
        if i == len(groups) - 1:
            core_rows, inner_grad, value = call(
                rows_kernel, "rows", [rows_shape, tile, joined], (grad_mid, inner_side, outer_side, chip_rows, inner_corner, outer_corner, *parts)
            )
            core_rows = paired(core_rows, "ty", "inner")
        elif i == 1:
            object_grad, value = call(
                columns_kernel,
                "columns",
                [tile, joined],
                (inner_grad, core_rows, *parts),
            )
        else:
            value = jnp.concatenate(parts, axis=0)
    other = paired(value, "ty", "inner")
    (probe_grad,) = call(join_kernel, "join", [shape(*probe_modes.shape)], (value, other))
    return (object_grad, probe_grad)


def solution(mesh):
    placed = (
        P(None, "ty", "tx"),
        P(),
        P("ty", "tx", None, None, None),
        P("ty", "tx", None, None),
        P(),
    )
    return jax.shard_map(
        shards, mesh=mesh, in_specs=placed, out_specs=(P(None, "ty", "tx"), P()), check_vma=False
    )
```

```python
import functools
import math

import jax
import jax.numpy as jnp
import ml_dtypes
import numpy as np
from jax import lax
from jax.experimental import pallas as pl
from jax.experimental.pallas import tpu as pltpu
from jax.sharding import PartitionSpec as P

FLOOR = 0.5
LANES = 128
CHUNK = 32
HEAVY = 200_000_000
VMEM_LIMIT = 28 * 1024 * 1024
SMALL_LIMIT = 8 * 1024 * 1024


def split_table(table):
    high = table.astype(ml_dtypes.bfloat16)
    low = (table - high.astype(np.float64)).astype(ml_dtypes.bfloat16)
    return high, low


def complex_block(matrix):
    return np.block([[matrix.real, matrix.imag], [-matrix.imag, matrix.real]])


@functools.lru_cache(maxsize=None)
def fourier_tables(pattern):
    half = pattern // 2
    n = np.arange(half)
    tables = []
    for parity in (0, 1):
        k = 2 * np.arange(half) + parity
        tables.append(np.exp(-2j * np.pi * ((n[:, None] * k[None, :]) % pattern) / pattern) / math.sqrt(pattern))
    forward = [complex_block(t) for t in tables]
    inverse = [complex_block(np.conj(t).T) for t in tables]
    every = forward + [t.T for t in forward] + [t.T for t in inverse] + inverse
    return np.stack([np.stack(split_table(t)) for t in every])


def split(value):
    high = value.astype(jnp.bfloat16)
    low = (value - high.astype(jnp.float32)).astype(jnp.bfloat16)
    return high, low


def mul(a, b):
    return jnp.dot(a, b, preferred_element_type=jnp.float32)


def near_and_far(unit):
    odd = lax.axis_index("ty") % 2
    return pl.multiple_of((1 - odd) * unit, LANES), pl.multiple_of(odd * unit, LANES)


def inner_and_outer():
    odd = lax.axis_index("tx") % 2
    return pl.multiple_of((1 - odd) * LANES, LANES), pl.multiple_of(odd * LANES, LANES)


def edges_kernel(field, center, chip_rows, sems):
    _, far = near_and_far(LANES)
    moves = ((field.at[:, pl.ds(far, LANES), :], chip_rows), (field, center))
    copies = [pltpu.make_async_copy(source, target, sems.at[i]) for i, (source, target) in enumerate(moves)]
    for copy in copies:
        copy.start()
    for copy in copies:
        copy.wait()


def sides_kernel(center, core_tile, inner_side, outer_side):
    half = LANES
    length = center.shape[1]
    odd = lax.axis_index("ty") % 2
    own, other = pl.multiple_of(odd * half, half), pl.multiple_of((1 - odd) * length, half)
    for target, start in zip((inner_side, outer_side), inner_and_outer()):
        cols = pl.ds(start, half)
        target[:, pl.ds(own, length), :] = center[:, :, cols]
        target[:, pl.ds(other, half), :] = core_tile[:, pl.ds(own, half), cols]


def corners_kernel(chip_rows, _, inner_corner, outer_corner):
    for target, start in zip((inner_corner, outer_corner), inner_and_outer()):
        target[...] = chip_rows[:, :, pl.ds(start, LANES)]


def root_kernel(measured, root, halves):
    pattern = measured.shape[2]
    source = lax.broadcasted_iota(jnp.int32, (pattern, pattern), 0)
    place = lax.broadcasted_iota(jnp.int32, (pattern, pattern), 1)
    half = pattern // 2
    wanted = jnp.where(place < half, 2 * place, 2 * (place - half) + 1)
    order = jnp.where(source == wanted, 1.0, 0.0).astype(jnp.bfloat16)
    for slot in range(measured.shape[0]):
        for b in range(2):
            halves[slot, b] = jnp.sqrt(measured[slot, :, b * LANES : (b + 1) * LANES])
        for parity in range(2):
            rows = pl.ds(parity, LANES, stride=2)
            high, low = split(jnp.concatenate([halves[slot, 0, rows, :], halves[slot, 1, rows, :]], axis=1))
            root[slot, parity] = mul(high, order) + mul(low, order)


def places_kernel(counts, spots, scalars):
    scalars[0] = counts[lax.axis_index("tx"), lax.axis_index("ty")]
    for slot in range(spots.shape[1]):
        for axis in range(2):
            scalars[1 + 2 * slot + axis] = spots[axis, slot]


def slots_kernel(
    scalars, center, core_tile, chip_rows, inner_side, outer_side, inner_corner, outer_corner, probe, root, tables,
    probe_sent, probe_keep, inner_side_out, outer_side_out, grad_mid,
    pad, grid, patch, rows_high, rows_low, freq, sums,
):
    half = LANES
    modes = probe.shape[1]
    length = center.shape[1]
    margin = chip_rows.shape[1]
    tall = inner_side.shape[1]
    near, far = near_and_far(margin + length)
    long_start = pl.multiple_of((1 - lax.axis_index("ty") % 2) * margin, half)
    near, far, both = pl.ds(near, margin), pl.ds(far, margin), pl.ds(long_start, tall)
    core_half = pl.ds(pl.multiple_of(lax.axis_index("ty") % 2 * half, half), half)
    inner = (1 - lax.axis_index("tx") % 2) * 3
    outer = 3 - inner

    for b in range(2):
        cols = slice(b * half, (b + 1) * half)
        pad[:, 1 + b, margin : margin + length, :] = center[:, :, cols]
        pad[:, 1 + b, near, :] = core_tile[:, core_half, cols]
        pad[:, 1 + b, far, :] = chip_rows[:, :, cols]
    pad[:, inner, both, :] = inner_side[...]
    pad[:, outer, both, :] = outer_side[...]
    pad[:, inner, far, :] = inner_corner[...]
    pad[:, outer, far, :] = outer_corner[...]
    grid[...] = jnp.zeros_like(grid)
    sums[...] = jnp.zeros_like(sums)
    lane = lax.broadcasted_iota(jnp.int32, (CHUNK, half), 1)

    def slot_step(slot, carry):
        row0 = scalars[1 + 2 * slot]
        col0 = scalars[2 + 2 * slot]
        block = jnp.minimum(col0 // half, 1)
        shift = col0 - block * half
        back_shift = lax.rem(half - shift, half)
        fore_shift = lax.rem(shift, half)

        for chunk in range(half // CHUNK):
            spectra = []
            for part in range(2):
                rows = part * half + chunk * CHUNK
                here = slice(rows, rows + CHUNK)
                cells = []
                for c in range(2):
                    rolled = [
                        pltpu.roll(pad[c, block + b, pl.ds(row0 + rows, CHUNK), :], back_shift, 1) for b in range(3)
                    ]
                    for b in range(2):
                        cell = jnp.where(lane < half - shift, rolled[b], rolled[b + 1])
                        patch[c, b, here, :] = cell
                        cells.append(cell)
                lefts = []
                for m in range(modes):
                    waves = []
                    for b in range(2):
                        pr = probe[0, m, here, b * half : (b + 1) * half]
                        pi = probe[1, m, here, b * half : (b + 1) * half]
                        waves.append((pr * cells[b] - pi * cells[2 + b], pr * cells[2 + b] + pi * cells[b]))
                    (ra, ia), (rb, ib) = waves
                    lefts.append((jnp.concatenate([ra + rb, ia + ib], axis=1), jnp.concatenate([ra - rb, ia - ib], axis=1)))
                spectra.append(lefts)
            for parity in range(2):
                stacked = jnp.concatenate([spectra[part][m][parity] for m in range(modes) for part in range(2)], axis=0)
                high, low = split(stacked)
                out = mul(jnp.concatenate([high, low, high], axis=1), jnp.concatenate([tables[parity, 0], tables[parity, 0], tables[parity, 1]], axis=0))
                for m in range(modes):
                    a = out[(2 * m) * CHUNK : (2 * m + 1) * CHUNK]
                    b = out[(2 * m + 1) * CHUNK : (2 * m + 2) * CHUNK]
                    for row_parity, value in enumerate((a + b, a - b)):
                        vh, vl = split(value)
                        for c in range(2):
                            at = slice(c * half + chunk * CHUNK, c * half + (chunk + 1) * CHUNK)
                            to = slice(parity * half, (parity + 1) * half)
                            rows_high[m, row_parity, at, to] = vh[:, c * half : (c + 1) * half]
                            rows_low[m, row_parity, at, to] = vl[:, c * half : (c + 1) * half]

        def row_transform(table, parity):
            for m in range(modes):
                high = rows_high[m, parity]
                low = rows_low[m, parity]
                freq[m, parity] = mul(
                    jnp.concatenate([tables[table + parity, 0], tables[table + parity, 1], tables[table + parity, 0]], axis=1),
                    jnp.concatenate([high, high, low], axis=0),
                )

        def apply_factor(parity):
            for chunk in range(half // CHUNK):
                real = slice(chunk * CHUNK, (chunk + 1) * CHUNK)
                imag = slice(half + chunk * CHUNK, half + (chunk + 1) * CHUNK)
                values = [(freq[m, parity, real, :], freq[m, parity, imag, :]) for m in range(modes)]
                power = sum(re * re + im * im for re, im in values)
                factor = 1.0 - root[slot, parity, real, :] * lax.rsqrt(jnp.maximum(power, FLOOR * FLOOR))
                for m in range(modes):
                    for at, value in zip((real, imag), values[m]):
                        vh, vl = split(value * factor)
                        rows_high[m, parity, at, :] = vh
                        rows_low[m, parity, at, :] = vl

        row_transform(2, 0)
        row_transform(2, 1)
        apply_factor(0)
        row_transform(4, 0)
        apply_factor(1)
        row_transform(4, 1)

        for chunk in range(half // CHUNK):
            real = slice(chunk * CHUNK, (chunk + 1) * CHUNK)
            imag = slice(half + chunk * CHUNK, half + (chunk + 1) * CHUNK)
            backs = []
            for q in range(2):
                cols = slice(q * half, (q + 1) * half)
                pieces = []
                for m in range(modes):
                    even = jnp.concatenate([freq[m, 0, real, cols], freq[m, 0, imag, cols]], axis=1)
                    odd = jnp.concatenate([freq[m, 1, real, cols], freq[m, 1, imag, cols]], axis=1)
                    pieces += [even + odd, even - odd]
                high, low = split(jnp.concatenate(pieces, axis=0))
                backs.append(mul(jnp.concatenate([high, low, high], axis=1), jnp.concatenate([tables[6 + q, 0], tables[6 + q, 0], tables[6 + q, 1]], axis=0)))
            halves = (backs[0] + backs[1], backs[0] - backs[1])
            for part in range(2):
                rows = part * half + chunk * CHUNK
                here = slice(rows, rows + CHUNK)
                total = [[0.0, 0.0], [0.0, 0.0]]
                for b in range(2):
                    xr = patch[0, b, here, :]
                    xi = patch[1, b, here, :]
                    for m in range(modes):
                        at = (2 * m + part) * CHUNK
                        br = halves[b][at : at + CHUNK, :half]
                        bi = halves[b][at : at + CHUNK, half:]
                        pr = probe[0, m, here, b * half : (b + 1) * half]
                        pi = probe[1, m, here, b * half : (b + 1) * half]
                        total[0][b] += pr * br + pi * bi
                        total[1][b] += pr * bi - pi * br
                        sums[pl.ds(((b * 2 + 0) * modes + m) * length + rows, CHUNK), :] += xr * br + xi * bi
                        sums[pl.ds(((b * 2 + 1) * modes + m) * length + rows, CHUNK), :] += xr * bi - xi * br
                for c in range(2):
                    ra = pltpu.roll(total[c][0], fore_shift, 1)
                    rb = pltpu.roll(total[c][1], fore_shift, 1)
                    beyond = lane >= shift
                    zero = jnp.zeros_like(ra)
                    placed = (jnp.where(beyond, ra, zero), jnp.where(beyond, rb, ra), jnp.where(beyond, zero, rb))
                    for b in range(3):
                        grid[c, block + b, pl.ds(row0 + rows, CHUNK), :] += placed[b]
        return carry

    lax.fori_loop(0, scalars[0], slot_step, 0)

    kept, rows, _ = probe_keep.shape
    code = own_code(digit_groups())

    def place_piece(place, carry):
        for first, target in ((0, probe_keep), (kept, probe_sent)):
            piece = (place + first) ^ code
            target[place] = sums[pl.ds(pl.multiple_of(piece * rows, rows), rows), :]
        return carry

    lax.fori_loop(0, kept, place_piece, 0)
    inner_side_out[...] = grid[:, inner]
    outer_side_out[...] = grid[:, outer]
    for b in range(2):
        grad_mid[:, :, b * half : (b + 1) * half] = grid[:, 1 + b]


def rows_kernel(grad_mid, inner_side, outer_side, _, core_out, chip_out, inner_grad):
    margin, length = core_out.shape[1], inner_grad.shape[1]
    near, far = (pl.ds(start, margin) for start in near_and_far(margin + length))
    for side, start in zip((inner_side, outer_side), inner_and_outer()):
        cols = pl.ds(start, LANES)
        for target, rows in ((core_out, near), (chip_out, far), (inner_grad, slice(margin, margin + length))):
            target[:, :, cols] = grad_mid[:, rows, cols] + side[:, rows, :]


def columns_kernel(inner_grad, core_in, chip_in, grad):
    near, far = (pl.ds(start, LANES) for start in near_and_far(LANES))
    grad[:, near, :] = inner_grad[:, near, :] + core_in[...]
    grad[:, far, :] = inner_grad[:, far, :] + chip_in[...]


def after_kernel(_, *refs):
    join_pieces(refs[:-1], refs[-1])


def join_pieces(pieces, joined):
    count = pieces[0].shape[0]
    for i, piece in enumerate(pieces):
        joined[i * count : (i + 1) * count] = piece[...]


def join_kernel(own, other, out):
    kept, rows, _ = own.shape
    _, modes, length, _ = out.shape
    code = own_code(digit_groups())
    each = length // rows

    for first, source in ((0, own), (kept, other)):

        def place_piece(place, carry, first=first, source=source):
            piece = (place + first) ^ code
            row = pl.multiple_of(piece % each * rows, rows)
            m = piece // each % modes
            c = piece // (each * modes) % 2
            b = pl.multiple_of(piece // (each * modes * 2) * LANES, LANES)
            out[c, m, pl.ds(row, rows), pl.ds(b, LANES)] = source[place]
            return carry

        lax.fori_loop(0, kept, place_piece, 0)


def exchanged(value, axis, mask):
    return lax.ppermute(value, axis, [(i, i ^ mask) for i in range(lax.axis_size(axis))])


def digit_groups():
    groups = [("ty", [1])]
    bits = [1 << i for i in range(1, lax.axis_size("ty").bit_length() - 1)]
    groups += [("ty", bits[i : i + 2]) for i in range(0, len(bits), 2)]
    return groups + [("tx", [1])]


def masks(bits):
    return [sum(bit for i, bit in enumerate(reversed(bits)) if j >> i & 1) for j in range(1 << len(bits))]


def own_code(groups):
    code = 0
    for axis, bits in groups:
        index = lax.axis_index(axis)
        for bit in bits:
            code = code * 2 + (index // bit) % 2
    return code


def pair_partner(index, kind):
    return index ^ 1 if kind == "inner" else index + 1 if index % 2 else index - 1


def paired(value, axis, kind):
    count = lax.axis_size(axis)
    pairs = [(i, pair_partner(i, kind)) for i in range(count)]
    return lax.ppermute(value, axis, [(i, j) for i, j in pairs if 0 <= j < count])


def add_kernel(scale, own, *refs):
    others, out = refs[:-1], refs[-1]
    count = out.shape[0]
    total = own[:count]
    for other in others:
        total += other[...]
    out[...] = total * scale


def added(own, others, scale=1.0, weight=0):
    out = jax.ShapeDtypeStruct(others[0].shape, jnp.float32)
    (result,) = call(functools.partial(add_kernel, scale), "add", [out], (own, *others), weight=weight)
    return result


def scattered(value, axis, bits):
    places = masks(bits)
    count = value.shape[0] // len(places)
    return [exchanged(value[j * count : (j + 1) * count], axis, places[j]) for j in range(1, len(places))]


def gathered(value, axis, bits):
    return [value] + [exchanged(value, axis, mask) for mask in masks(bits)[1:]]


def call(body, name, out, operands, spaces="", results="", scratch=(), limit=SMALL_LIMIT, weight=0):
    kinds = {"v": pltpu.VMEM, "s": pltpu.SMEM, "h": pltpu.HBM}

    def specs(letters, count):
        return tuple(pl.BlockSpec(memory_space=kinds[x]) for x in letters + "v" * (count - len(letters)))

    moved = weight + sum(math.prod(v.shape) * v.dtype.itemsize for v in tuple(operands) + tuple(out))
    return pl.pallas_call(
        body,
        out_shape=tuple(out),
        in_specs=specs(spaces, len(operands)),
        out_specs=specs(results, len(out)),
        scratch_shapes=list(scratch),
        compiler_params=pltpu.CompilerParams(vmem_limit_bytes=limit),
        cost_estimate=pl.CostEstimate(flops=0, bytes_accessed=moved, transcendentals=0),
        name=name,
    )(*operands)


def shards(object_field, probe_modes, intensities, offsets, counts):
    length = object_field.shape[1]
    modes, pattern = probe_modes.shape[1:3]
    margin = pattern // 2
    half = LANES
    devices = lax.axis_size("ty") * lax.axis_size("tx")
    groups = digit_groups()
    f32, bf16 = jnp.float32, jnp.bfloat16
    slots = intensities.shape[2]
    tables = jnp.asarray(fourier_tables(pattern))

    def shape(*sizes):
        return jax.ShapeDtypeStruct(sizes, f32)

    tile, rows_shape = shape(2, length, length), shape(2, margin, length)
    side, tall_side, corner = shape(2, length + margin, margin), shape(2, length + 2 * margin, margin), shape(2, margin, margin)
    core_tile = paired(object_field, "ty", "inner")
    center, chip_rows = call(
        edges_kernel, "edges", [tile, rows_shape], (object_field,), "h", scratch=(pltpu.SemaphoreType.DMA((2,)),)
    )
    chip_rows = paired(chip_rows, "ty", "outer")
    inner_side, outer_side = call(sides_kernel, "sides", [side, side], (center, core_tile))
    inner_side = paired(inner_side, "tx", "inner")
    outer_side = paired(outer_side, "tx", "outer")
    (root,) = call(
        root_kernel,
        "root",
        [shape(slots, 2, half, pattern)],
        (intensities[0, 0],),
        scratch=(pltpu.VMEM((slots, 2, pattern, half), f32),),
    )
    inner_corner, outer_corner = call(corners_kernel, "corners", [corner, corner], (chip_rows, root), "vh")
    inner_corner = paired(inner_corner, "tx", "inner")
    outer_corner = paired(outer_corner, "tx", "outer")
    (scalars,) = call(
        places_kernel, "places", [jax.ShapeDtypeStruct((1 + 2 * slots,), jnp.int32)], (counts.T, offsets[0, 0].T), "ss", "s"
    )

    pieces = 1 << sum(len(bits) for _, bits in groups)
    rows = 2 * 2 * modes * pattern // pieces
    kept = shape(pieces // 2, rows, half)
    probe_sent, value, inner_side, outer_side, grad_mid = call(
        slots_kernel,
        "slots",
        [kept, kept, tall_side, tall_side, shape(2, length + 2 * margin, length)],
        (scalars, center, core_tile, chip_rows, inner_side, outer_side, inner_corner, outer_corner, probe_modes, root, tables),
        "s",
        scratch=(
            pltpu.VMEM((2, 4, length + 2 * margin, half), f32),
            pltpu.VMEM((2, 4, length + 2 * margin, half), f32),
            pltpu.VMEM((2, 2, pattern, half), f32),
            pltpu.VMEM((modes, 2, pattern, pattern), bf16),
            pltpu.VMEM((modes, 2, pattern, pattern), bf16),
            pltpu.VMEM((modes, 2, pattern, pattern), f32),
            pltpu.VMEM((2 * 2 * modes * pattern, half), f32),
        ),
        limit=VMEM_LIMIT,
    )

    value = added(value, [paired(probe_sent, "ty", "inner")], weight=HEAVY)
    inner_side = paired(inner_side, "tx", "inner")
    outer_side = paired(outer_side, "tx", "outer")
    for group in groups[1:-1]:
        value = added(value, scattered(value, *group))
    value = added(value, scattered(value, *groups[-1]), scale=1.0 / devices)
    core_rows, chip_rows, inner_grad = call(
        rows_kernel,
        "rows",
        [rows_shape, rows_shape, tile],
        (grad_mid, inner_side, outer_side, value),
        "vvvh",
        weight=HEAVY,
    )
    chip_rows = paired(chip_rows, "ty", "outer")
    core_rows = paired(core_rows, "ty", "inner")
    for i in range(1, lax.axis_size("tx").bit_length() - 1):
        value = added(value, [exchanged(value, "tx", 1 << i)])
    for i in range(len(groups) - 1, 0, -1):
        parts = gathered(value, *groups[i])
        joined = shape(len(parts) * value.shape[0], rows, half)
        arrived = chip_rows if i == len(groups) - 1 else core_rows
        (value,) = call(after_kernel, "after", [joined], (arrived, *parts), "h")
    (object_grad,) = call(columns_kernel, "columns", [tile], (inner_grad, core_rows, chip_rows))
    other = paired(value, "ty", "inner")
    (probe_grad,) = call(join_kernel, "join", [shape(*probe_modes.shape)], (value, other))
    return (object_grad, probe_grad)


def solution(mesh):
    placed = (
        P(None, "ty", "tx"),
        P(),
        P("ty", "tx", None, None, None),
        P("ty", "tx", None, None),
        P(),
    )
    return jax.shard_map(
        shards, mesh=mesh, in_specs=placed, out_specs=(P(None, "ty", "tx"), P()), check_vma=False
    )
```

```python
import functools
import math

import jax
import jax.numpy as jnp
import ml_dtypes
import numpy as np
from jax import lax
from jax.experimental import pallas as pl
from jax.experimental.pallas import tpu as pltpu
from jax.sharding import PartitionSpec as P

FLOOR = 0.5
LANES = 128
CHUNK = 32
HEAVY = 0
AHEAD = 4_000_000_000
AROUND = 2_000_000_000
VMEM_LIMIT = 28 * 1024 * 1024
SMALL_LIMIT = 8 * 1024 * 1024


def split_table(table):
    high = table.astype(ml_dtypes.bfloat16)
    low = (table - high.astype(np.float64)).astype(ml_dtypes.bfloat16)
    return high, low


def complex_block(matrix):
    return np.block([[matrix.real, matrix.imag], [-matrix.imag, matrix.real]])


@functools.lru_cache(maxsize=None)
def fourier_tables(pattern):
    half = pattern // 2
    n = np.arange(half)
    tables = []
    for parity in (0, 1):
        k = 2 * np.arange(half) + parity
        tables.append(np.exp(-2j * np.pi * ((n[:, None] * k[None, :]) % pattern) / pattern) / math.sqrt(pattern))
    forward = [complex_block(t) for t in tables]
    inverse = [complex_block(np.conj(t).T) for t in tables]
    every = forward + [t.T for t in forward] + [t.T for t in inverse] + inverse
    return np.stack([np.stack(split_table(t)) for t in every])


def split(value):
    high = value.astype(jnp.bfloat16)
    low = (value - high.astype(jnp.float32)).astype(jnp.bfloat16)
    return high, low


def mul(a, b):
    return jnp.dot(a, b, preferred_element_type=jnp.float32)


def near_and_far(unit):
    odd = lax.axis_index("ty") % 2
    return pl.multiple_of((1 - odd) * unit, LANES), pl.multiple_of(odd * unit, LANES)


def inner_and_outer():
    odd = lax.axis_index("tx") % 2
    return pl.multiple_of((1 - odd) * LANES, LANES), pl.multiple_of(odd * LANES, LANES)


def edges_kernel(field, center, chip_rows, inner_side, outer_side, sems):
    _, far = near_and_far(LANES)
    inner, outer = inner_and_outer()
    moves = (
        (field.at[:, pl.ds(far, LANES), :], chip_rows),
        (field.at[:, :, pl.ds(inner, LANES)], inner_side),
        (field.at[:, :, pl.ds(outer, LANES)], outer_side),
        (field, center),
    )
    copies = [pltpu.make_async_copy(source, target, sems.at[i]) for i, (source, target) in enumerate(moves)]
    for copy in copies:
        copy.start()
    for copy in copies:
        copy.wait()


def near_kernel(inner_side, outer_side, inner_near, outer_near):
    near, _ = near_and_far(LANES)
    inner_near[...] = inner_side[:, pl.ds(near, LANES), :]
    outer_near[...] = outer_side[:, pl.ds(near, LANES), :]


def far_kernel(chip_rows, inner_corner, outer_corner, far_rows):
    inner = (1 - lax.axis_index("tx") % 2) * 3
    for b in range(2):
        far_rows[:, 1 + b] = chip_rows[:, :, b * LANES : (b + 1) * LANES]
    far_rows[:, inner] = inner_corner[...]
    far_rows[:, 3 - inner] = outer_corner[...]


def corners_kernel(chip_rows, _, __, inner_corner, outer_corner):
    for target, start in zip((inner_corner, outer_corner), inner_and_outer()):
        target[...] = chip_rows[:, :, pl.ds(start, LANES)]


def root_kernel(measured, root, halves):
    pattern = measured.shape[2]
    source = lax.broadcasted_iota(jnp.int32, (pattern, pattern), 0)
    place = lax.broadcasted_iota(jnp.int32, (pattern, pattern), 1)
    half = pattern // 2
    wanted = jnp.where(place < half, 2 * place, 2 * (place - half) + 1)
    order = jnp.where(source == wanted, 1.0, 0.0).astype(jnp.bfloat16)
    for slot in range(measured.shape[0]):
        for b in range(2):
            halves[slot, b] = jnp.sqrt(measured[slot, :, b * LANES : (b + 1) * LANES])
        for parity in range(2):
            rows = pl.ds(parity, LANES, stride=2)
            high, low = split(jnp.concatenate([halves[slot, 0, rows, :], halves[slot, 1, rows, :]], axis=1))
            root[slot, parity] = mul(high, order) + mul(low, order)


def places_kernel(counts, spots, scalars):
    scalars[0] = counts[lax.axis_index("tx"), lax.axis_index("ty")]
    for slot in range(spots.shape[1]):
        for axis in range(2):
            scalars[1 + 2 * slot + axis] = spots[axis, slot]


def slots_kernel(
    scalars, center, core_tile, far_rows, inner_side, outer_side, inner_near, outer_near, probe, root, tables,
    probe_sent, probe_keep, inner_side_out, outer_side_out, grad_mid,
    pad, grid, patch, rows_high, rows_low, freq, sums,
):
    half = LANES
    modes = probe.shape[1]
    length = center.shape[1]
    margin = far_rows.shape[2]
    near, far = near_and_far(margin + length)
    near, far, own = pl.ds(near, margin), pl.ds(far, margin), pl.ds(margin, length)
    core_half = pl.ds(pl.multiple_of(lax.axis_index("ty") % 2 * half, half), half)
    inner = (1 - lax.axis_index("tx") % 2) * 3
    outer = 3 - inner

    for b in range(2):
        cols = slice(b * half, (b + 1) * half)
        pad[:, 1 + b, margin : margin + length, :] = center[:, :, cols]
        pad[:, 1 + b, near, :] = core_tile[:, core_half, cols]
    pad[:, inner, own, :] = inner_side[...]
    pad[:, outer, own, :] = outer_side[...]
    pad[:, inner, near, :] = inner_near[...]
    pad[:, outer, near, :] = outer_near[...]
    pad[:, :, far, :] = far_rows[...]
    grid[...] = jnp.zeros_like(grid)
    sums[...] = jnp.zeros_like(sums)
    lane = lax.broadcasted_iota(jnp.int32, (CHUNK, half), 1)

    def slot_step(slot, carry):
        row0 = scalars[1 + 2 * slot]
        col0 = scalars[2 + 2 * slot]
        block = jnp.minimum(col0 // half, 1)
        shift = col0 - block * half
        back_shift = lax.rem(half - shift, half)
        fore_shift = lax.rem(shift, half)

        for chunk in range(half // CHUNK):
            spectra = []
            for part in range(2):
                rows = part * half + chunk * CHUNK
                here = slice(rows, rows + CHUNK)
                cells = []
                for c in range(2):
                    rolled = [
                        pltpu.roll(pad[c, block + b, pl.ds(row0 + rows, CHUNK), :], back_shift, 1) for b in range(3)
                    ]
                    for b in range(2):
                        cell = jnp.where(lane < half - shift, rolled[b], rolled[b + 1])
                        patch[c, b, here, :] = cell
                        cells.append(cell)
                lefts = []
                for m in range(modes):
                    waves = []
                    for b in range(2):
                        pr = probe[0, m, here, b * half : (b + 1) * half]
                        pi = probe[1, m, here, b * half : (b + 1) * half]
                        waves.append((pr * cells[b] - pi * cells[2 + b], pr * cells[2 + b] + pi * cells[b]))
                    (ra, ia), (rb, ib) = waves
                    lefts.append((jnp.concatenate([ra + rb, ia + ib], axis=1), jnp.concatenate([ra - rb, ia - ib], axis=1)))
                spectra.append(lefts)
            for parity in range(2):
                stacked = jnp.concatenate([spectra[part][m][parity] for m in range(modes) for part in range(2)], axis=0)
                high, low = split(stacked)
                out = mul(jnp.concatenate([high, low, high], axis=1), jnp.concatenate([tables[parity, 0], tables[parity, 0], tables[parity, 1]], axis=0))
                for m in range(modes):
                    a = out[(2 * m) * CHUNK : (2 * m + 1) * CHUNK]
                    b = out[(2 * m + 1) * CHUNK : (2 * m + 2) * CHUNK]
                    for row_parity, value in enumerate((a + b, a - b)):
                        vh, vl = split(value)
                        for c in range(2):
                            at = slice(c * half + chunk * CHUNK, c * half + (chunk + 1) * CHUNK)
                            to = slice(parity * half, (parity + 1) * half)
                            rows_high[m, row_parity, at, to] = vh[:, c * half : (c + 1) * half]
                            rows_low[m, row_parity, at, to] = vl[:, c * half : (c + 1) * half]

        def row_transform(table, parity):
            for m in range(modes):
                high = rows_high[m, parity]
                low = rows_low[m, parity]
                freq[m, parity] = mul(
                    jnp.concatenate([tables[table + parity, 0], tables[table + parity, 1], tables[table + parity, 0]], axis=1),
                    jnp.concatenate([high, high, low], axis=0),
                )

        def apply_factor(parity):
            for chunk in range(half // CHUNK):
                real = slice(chunk * CHUNK, (chunk + 1) * CHUNK)
                imag = slice(half + chunk * CHUNK, half + (chunk + 1) * CHUNK)
                values = [(freq[m, parity, real, :], freq[m, parity, imag, :]) for m in range(modes)]
                power = sum(re * re + im * im for re, im in values)
                factor = 1.0 - root[slot, parity, real, :] * lax.rsqrt(jnp.maximum(power, FLOOR * FLOOR))
                for m in range(modes):
                    for at, value in zip((real, imag), values[m]):
                        vh, vl = split(value * factor)
                        rows_high[m, parity, at, :] = vh
                        rows_low[m, parity, at, :] = vl

        row_transform(2, 0)
        row_transform(2, 1)
        apply_factor(0)
        row_transform(4, 0)
        apply_factor(1)
        row_transform(4, 1)

        for chunk in range(half // CHUNK):
            real = slice(chunk * CHUNK, (chunk + 1) * CHUNK)
            imag = slice(half + chunk * CHUNK, half + (chunk + 1) * CHUNK)
            backs = []
            for q in range(2):
                cols = slice(q * half, (q + 1) * half)
                pieces = []
                for m in range(modes):
                    even = jnp.concatenate([freq[m, 0, real, cols], freq[m, 0, imag, cols]], axis=1)
                    odd = jnp.concatenate([freq[m, 1, real, cols], freq[m, 1, imag, cols]], axis=1)
                    pieces += [even + odd, even - odd]
                high, low = split(jnp.concatenate(pieces, axis=0))
                backs.append(mul(jnp.concatenate([high, low, high], axis=1), jnp.concatenate([tables[6 + q, 0], tables[6 + q, 0], tables[6 + q, 1]], axis=0)))
            halves = (backs[0] + backs[1], backs[0] - backs[1])
            for part in range(2):
                rows = part * half + chunk * CHUNK
                here = slice(rows, rows + CHUNK)
                total = [[0.0, 0.0], [0.0, 0.0]]
                for b in range(2):
                    xr = patch[0, b, here, :]
                    xi = patch[1, b, here, :]
                    for m in range(modes):
                        at = (2 * m + part) * CHUNK
                        br = halves[b][at : at + CHUNK, :half]
                        bi = halves[b][at : at + CHUNK, half:]
                        pr = probe[0, m, here, b * half : (b + 1) * half]
                        pi = probe[1, m, here, b * half : (b + 1) * half]
                        total[0][b] += pr * br + pi * bi
                        total[1][b] += pr * bi - pi * br
                        sums[pl.ds(((b * 2 + 0) * modes + m) * length + rows, CHUNK), :] += xr * br + xi * bi
                        sums[pl.ds(((b * 2 + 1) * modes + m) * length + rows, CHUNK), :] += xr * bi - xi * br
                for c in range(2):
                    ra = pltpu.roll(total[c][0], fore_shift, 1)
                    rb = pltpu.roll(total[c][1], fore_shift, 1)
                    beyond = lane >= shift
                    zero = jnp.zeros_like(ra)
                    placed = (jnp.where(beyond, ra, zero), jnp.where(beyond, rb, ra), jnp.where(beyond, zero, rb))
                    for b in range(3):
                        grid[c, block + b, pl.ds(row0 + rows, CHUNK), :] += placed[b]
        return carry

    lax.fori_loop(0, scalars[0], slot_step, 0)

    kept, rows, _ = probe_keep.shape
    code = own_code(digit_groups())

    def place_piece(place, carry):
        for first, target in ((0, probe_keep), (kept, probe_sent)):
            piece = (place + first) ^ code
            target[place] = sums[pl.ds(pl.multiple_of(piece * rows, rows), rows), :]
        return carry

    lax.fori_loop(0, kept, place_piece, 0)
    inner_side_out[...] = grid[:, inner]
    outer_side_out[...] = grid[:, outer]
    for b in range(2):
        grad_mid[:, :, b * half : (b + 1) * half] = grid[:, 1 + b]


def rows_kernel(grad_mid, inner_side, outer_side, _, core_out, chip_out, inner_grad):
    margin, length = core_out.shape[1], inner_grad.shape[1]
    near, far = (pl.ds(start, margin) for start in near_and_far(margin + length))
    for side, start in zip((inner_side, outer_side), inner_and_outer()):
        cols = pl.ds(start, LANES)
        for target, rows in ((core_out, near), (chip_out, far), (inner_grad, slice(margin, margin + length))):
            target[:, :, cols] = grad_mid[:, rows, cols] + side[:, rows, :]


def columns_kernel(inner_grad, core_in, chip_in, grad):
    near, far = (pl.ds(start, LANES) for start in near_and_far(LANES))
    grad[:, near, :] = inner_grad[:, near, :] + core_in[...]
    grad[:, far, :] = inner_grad[:, far, :] + chip_in[...]


def after_kernel(_, *refs):
    join_pieces(refs[:-1], refs[-1])


def join_pieces(pieces, joined):
    count = pieces[0].shape[0]
    for i, piece in enumerate(pieces):
        joined[i * count : (i + 1) * count] = piece[...]


def join_kernel(first, *refs):
    source, out, sems = refs[0], refs[-2], refs[-1]
    kept, rows, _ = source.shape
    _, modes, length, _ = out.shape
    code = own_code(digit_groups())
    each = length // rows
    copies = []
    for place in range(kept):
        piece = (place + first) ^ code
        row = pl.multiple_of(piece % each * rows, rows)
        m = piece // each % modes
        c = piece // (each * modes) % 2
        b = pl.multiple_of(piece // (each * modes * 2) * LANES, LANES)
        copies.append(
            pltpu.make_async_copy(source.at[place], out.at[c, m, pl.ds(row, rows), pl.ds(b, LANES)], sems.at[place])
        )
    for copy in copies:
        copy.start()
    for copy in copies:
        copy.wait()


def exchanged(value, axis, mask):
    return lax.ppermute(value, axis, [(i, i ^ mask) for i in range(lax.axis_size(axis))])


def digit_groups():
    groups = [("ty", [1])]
    bits = [1 << i for i in range(1, lax.axis_size("ty").bit_length() - 1)]
    groups += [("ty", bits[i : i + 2]) for i in range(0, len(bits), 2)]
    return groups + [("tx", [1])]


def masks(bits):
    return [sum(bit for i, bit in enumerate(reversed(bits)) if j >> i & 1) for j in range(1 << len(bits))]


def own_code(groups):
    code = 0
    for axis, bits in groups:
        index = lax.axis_index(axis)
        for bit in bits:
            code = code * 2 + (index // bit) % 2
    return code


def pair_partner(index, kind):
    return index ^ 1 if kind == "inner" else index + 1 if index % 2 else index - 1


def paired(value, axis, kind):
    count = lax.axis_size(axis)
    pairs = [(i, pair_partner(i, kind)) for i in range(count)]
    return lax.ppermute(value, axis, [(i, j) for i, j in pairs if 0 <= j < count])


def add_kernel(scale, own, *refs):
    others, out = refs[:-1], refs[-1]
    count = out.shape[0]
    total = own[:count]
    for other in others:
        total += other[...]
    out[...] = total * scale


def added(own, others, scale=1.0, weight=0):
    out = jax.ShapeDtypeStruct(others[0].shape, jnp.float32)
    (result,) = call(functools.partial(add_kernel, scale), "add", [out], (own, *others), weight=weight)
    return result


def scattered(value, axis, bits):
    places = masks(bits)
    count = value.shape[0] // len(places)
    return [exchanged(value[j * count : (j + 1) * count], axis, places[j]) for j in range(1, len(places))]


def gathered(value, axis, bits):
    return [value] + [exchanged(value, axis, mask) for mask in masks(bits)[1:]]


def call(body, name, out, operands, spaces="", results="", scratch=(), limit=SMALL_LIMIT, weight=0, aliases=None):
    kinds = {"v": pltpu.VMEM, "s": pltpu.SMEM, "h": pltpu.HBM}

    def specs(letters, count):
        return tuple(pl.BlockSpec(memory_space=kinds[x]) for x in letters + "v" * (count - len(letters)))

    moved = sum(math.prod(v.shape) * v.dtype.itemsize for v in tuple(operands) + tuple(out))
    return pl.pallas_call(
        body,
        out_shape=tuple(out),
        in_specs=specs(spaces, len(operands)),
        out_specs=specs(results, len(out)),
        scratch_shapes=list(scratch),
        input_output_aliases=aliases or {},
        compiler_params=pltpu.CompilerParams(vmem_limit_bytes=limit),
        cost_estimate=pl.CostEstimate(flops=weight, bytes_accessed=moved, transcendentals=0),
        name=name,
    )(*operands)


def shards(object_field, probe_modes, intensities, offsets, counts):
    length = object_field.shape[1]
    modes, pattern = probe_modes.shape[1:3]
    margin = pattern // 2
    half = LANES
    devices = lax.axis_size("ty") * lax.axis_size("tx")
    groups = digit_groups()
    f32, bf16 = jnp.float32, jnp.bfloat16
    slots = intensities.shape[2]
    tables = jnp.asarray(fourier_tables(pattern))

    def shape(*sizes):
        return jax.ShapeDtypeStruct(sizes, f32)

    tile, rows_shape = shape(2, length, length), shape(2, margin, length)
    side, tall_side, corner = shape(2, length, margin), shape(2, length + 2 * margin, margin), shape(2, margin, margin)
    core_tile = paired(object_field, "ty", "inner")
    center, chip_rows, inner_side, outer_side = call(
        edges_kernel, "edges", [tile, rows_shape, side, side], (object_field,), "h", scratch=(pltpu.SemaphoreType.DMA((4,)),)
    )
    chip_rows = paired(chip_rows, "ty", "outer")
    inner_side = paired(inner_side, "tx", "inner")
    outer_side = paired(outer_side, "tx", "outer")
    (root,) = call(
        root_kernel,
        "root",
        [shape(slots, 2, half, pattern)],
        (intensities[0, 0],),
        scratch=(pltpu.VMEM((slots, 2, pattern, half), f32),),
        weight=AROUND,
    )
    (scalars,) = call(
        places_kernel, "places", [jax.ShapeDtypeStruct((1 + 2 * slots,), jnp.int32)], (counts.T, offsets[0, 0].T), "ss", "s", weight=AROUND
    )
    inner_corner, outer_corner = call(corners_kernel, "corners", [corner, corner], (chip_rows, root, scalars), "vhh")
    inner_corner = paired(inner_corner, "tx", "inner")
    outer_corner = paired(outer_corner, "tx", "outer")
    inner_near, outer_near = call(near_kernel, "near", [corner, corner], (inner_side, outer_side))
    inner_near = paired(inner_near, "ty", "inner")
    outer_near = paired(outer_near, "ty", "inner")
    (far_rows,) = call(far_kernel, "far", [shape(2, 4, margin, half)], (chip_rows, inner_corner, outer_corner), weight=AHEAD)
    pieces = 1 << sum(len(bits) for _, bits in groups)
    rows = 2 * 2 * modes * pattern // pieces
    kept = shape(pieces // 2, rows, half)
    probe_sent, value, inner_side, outer_side, grad_mid = call(
        slots_kernel,
        "slots",
        [kept, kept, tall_side, tall_side, shape(2, length + 2 * margin, length)],
        (
            scalars, center, core_tile, far_rows, inner_side, outer_side, inner_near, outer_near,
            probe_modes, root, tables,
        ),
        "s",
        scratch=(
            pltpu.VMEM((2, 4, length + 2 * margin, half), f32),
            pltpu.VMEM((2, 4, length + 2 * margin, half), f32),
            pltpu.VMEM((2, 2, pattern, half), f32),
            pltpu.VMEM((modes, 2, pattern, pattern), bf16),
            pltpu.VMEM((modes, 2, pattern, pattern), bf16),
            pltpu.VMEM((modes, 2, pattern, pattern), f32),
            pltpu.VMEM((2 * 2 * modes * pattern, half), f32),
        ),
        limit=VMEM_LIMIT,
    )

    value = added(value, [paired(probe_sent, "ty", "inner")], weight=HEAVY)
    inner_side = paired(inner_side, "tx", "inner")
    outer_side = paired(outer_side, "tx", "outer")
    for group in groups[1:-1]:
        value = added(value, scattered(value, *group))
    value = added(value, scattered(value, *groups[-1]), scale=1.0 / devices)
    core_rows, chip_rows, inner_grad = call(
        rows_kernel,
        "rows",
        [rows_shape, rows_shape, tile],
        (grad_mid, inner_side, outer_side, value),
        "vvvh",
        weight=HEAVY,
    )
    chip_rows = paired(chip_rows, "ty", "outer")
    core_rows = paired(core_rows, "ty", "inner")
    for i in range(1, lax.axis_size("tx").bit_length() - 1):
        value = added(value, [exchanged(value, "tx", 1 << i)])
    for i in range(len(groups) - 1, 0, -1):
        parts = gathered(value, *groups[i])
        joined = shape(len(parts) * value.shape[0], rows, half)
        arrived = chip_rows if i == len(groups) - 1 else core_rows
        (value,) = call(after_kernel, "after", [joined], (arrived, *parts), "h")
    (object_grad,) = call(columns_kernel, "columns", [tile], (inner_grad, core_rows, chip_rows))
    other = paired(value, "ty", "inner")
    sems = (pltpu.SemaphoreType.DMA((pieces // 2,)),)
    (probe_grad,) = call(
        functools.partial(join_kernel, 0), "join", [shape(*probe_modes.shape)], (value,), "v", "h", sems, weight=AROUND
    )
    (probe_grad,) = call(
        functools.partial(join_kernel, pieces // 2),
        "join_rest",
        [shape(*probe_modes.shape)],
        (other, probe_grad),
        "vh",
        "h",
        sems,
        aliases={1: 0},
    )
    return (object_grad, probe_grad)


def solution(mesh):
    placed = (
        P(None, "ty", "tx"),
        P(),
        P("ty", "tx", None, None, None),
        P("ty", "tx", None, None),
        P(),
    )
    return jax.shard_map(
        shards, mesh=mesh, in_specs=placed, out_specs=(P(None, "ty", "tx"), P()), check_vma=False
    )
```

```python
import functools
import math

import jax
import jax.numpy as jnp
import ml_dtypes
import numpy as np
from jax import lax
from jax.experimental import pallas as pl
from jax.experimental.pallas import tpu as pltpu
from jax.sharding import PartitionSpec as P

FLOOR = 0.5
LANES = 128
CHUNK = 32
HEAVY = 0
AHEAD = 4_000_000_000
AROUND = 2_000_000_000
VMEM_LIMIT = 28 * 1024 * 1024
SMALL_LIMIT = 8 * 1024 * 1024


def split_table(table):
    high = table.astype(ml_dtypes.bfloat16)
    low = (table - high.astype(np.float64)).astype(ml_dtypes.bfloat16)
    return high, low


def complex_block(matrix):
    return np.block([[matrix.real, matrix.imag], [-matrix.imag, matrix.real]])


@functools.lru_cache(maxsize=None)
def fourier_tables(pattern):
    half = pattern // 2
    n = np.arange(half)
    tables = []
    for parity in (0, 1):
        k = 2 * np.arange(half) + parity
        tables.append(np.exp(-2j * np.pi * ((n[:, None] * k[None, :]) % pattern) / pattern) / math.sqrt(pattern))
    forward = [complex_block(t) for t in tables]
    inverse = [complex_block(np.conj(t).T) for t in tables]
    every = forward + [t.T for t in forward] + [t.T for t in inverse] + inverse
    return np.stack([np.stack(split_table(t)) for t in every])


def split(value):
    high = value.astype(jnp.bfloat16)
    low = (value - high.astype(jnp.float32)).astype(jnp.bfloat16)
    return high, low


def mul(a, b):
    return jnp.dot(a, b, preferred_element_type=jnp.float32)


def near_and_far(unit):
    odd = lax.axis_index("ty") % 2
    return pl.multiple_of((1 - odd) * unit, LANES), pl.multiple_of(odd * unit, LANES)


def inner_and_outer():
    odd = lax.axis_index("tx") % 2
    return pl.multiple_of((1 - odd) * LANES, LANES), pl.multiple_of(odd * LANES, LANES)


def chip_edges_kernel(field, chip_rows, sem):
    _, far = near_and_far(LANES)
    copy = pltpu.make_async_copy(field.at[:, pl.ds(far, LANES), :], chip_rows, sem)
    copy.start()
    copy.wait()


def edges_kernel(field, _, center, inner_side, outer_side, sems):
    inner, outer = inner_and_outer()
    moves = (
        (field.at[:, :, pl.ds(inner, LANES)], inner_side),
        (field.at[:, :, pl.ds(outer, LANES)], outer_side),
        (field, center),
    )
    copies = [pltpu.make_async_copy(source, target, sems.at[i]) for i, (source, target) in enumerate(moves)]
    for copy in copies:
        copy.start()
    for copy in copies:
        copy.wait()


def near_kernel(inner_side, outer_side, inner_near, outer_near):
    near, _ = near_and_far(LANES)
    inner_near[...] = inner_side[:, pl.ds(near, LANES), :]
    outer_near[...] = outer_side[:, pl.ds(near, LANES), :]


def far_kernel(chip_rows, inner_corner, outer_corner, far_rows):
    inner = (1 - lax.axis_index("tx") % 2) * 3
    for b in range(2):
        far_rows[:, 1 + b] = chip_rows[:, :, b * LANES : (b + 1) * LANES]
    far_rows[:, inner] = inner_corner[...]
    far_rows[:, 3 - inner] = outer_corner[...]


def corners_kernel(chip_rows, _, __, inner_corner, outer_corner):
    for target, start in zip((inner_corner, outer_corner), inner_and_outer()):
        target[...] = chip_rows[:, :, pl.ds(start, LANES)]


def root_kernel(measured, root, halves):
    pattern = measured.shape[2]
    source = lax.broadcasted_iota(jnp.int32, (pattern, pattern), 0)
    place = lax.broadcasted_iota(jnp.int32, (pattern, pattern), 1)
    half = pattern // 2
    wanted = jnp.where(place < half, 2 * place, 2 * (place - half) + 1)
    order = jnp.where(source == wanted, 1.0, 0.0).astype(jnp.bfloat16)
    for slot in range(measured.shape[0]):
        for b in range(2):
            halves[slot, b] = jnp.sqrt(measured[slot, :, b * LANES : (b + 1) * LANES])
        for parity in range(2):
            rows = pl.ds(parity, LANES, stride=2)
            high, low = split(jnp.concatenate([halves[slot, 0, rows, :], halves[slot, 1, rows, :]], axis=1))
            root[slot, parity] = mul(high, order) + mul(low, order)


def places_kernel(counts, spots, scalars):
    scalars[0] = counts[lax.axis_index("tx"), lax.axis_index("ty")]
    for slot in range(spots.shape[1]):
        for axis in range(2):
            scalars[1 + 2 * slot + axis] = spots[axis, slot]


def slots_kernel(
    scalars, center, core_tile, far_rows, inner_side, outer_side, inner_near, outer_near, probe, root, tables,
    probe_sent, probe_keep, inner_side_out, outer_side_out, grad_mid,
    pad, grid, patch, rows_high, rows_low, freq, sums,
):
    half = LANES
    modes = probe.shape[1]
    length = center.shape[1]
    margin = far_rows.shape[2]
    near, far = near_and_far(margin + length)
    near, far, own = pl.ds(near, margin), pl.ds(far, margin), pl.ds(margin, length)
    core_half = pl.ds(pl.multiple_of(lax.axis_index("ty") % 2 * half, half), half)
    inner = (1 - lax.axis_index("tx") % 2) * 3
    outer = 3 - inner

    for b in range(2):
        cols = slice(b * half, (b + 1) * half)
        pad[:, 1 + b, margin : margin + length, :] = center[:, :, cols]
        pad[:, 1 + b, near, :] = core_tile[:, core_half, cols]
    pad[:, inner, own, :] = inner_side[...]
    pad[:, outer, own, :] = outer_side[...]
    pad[:, inner, near, :] = inner_near[...]
    pad[:, outer, near, :] = outer_near[...]
    pad[:, :, far, :] = far_rows[...]
    grid[...] = jnp.zeros_like(grid)
    sums[...] = jnp.zeros_like(sums)
    lane = lax.broadcasted_iota(jnp.int32, (CHUNK, half), 1)

    def slot_step(slot, carry):
        row0 = scalars[1 + 2 * slot]
        col0 = scalars[2 + 2 * slot]
        block = jnp.minimum(col0 // half, 1)
        shift = col0 - block * half
        back_shift = lax.rem(half - shift, half)
        fore_shift = lax.rem(shift, half)

        for chunk in range(half // CHUNK):
            spectra = []
            for part in range(2):
                rows = part * half + chunk * CHUNK
                here = slice(rows, rows + CHUNK)
                cells = []
                for c in range(2):
                    rolled = [
                        pltpu.roll(pad[c, block + b, pl.ds(row0 + rows, CHUNK), :], back_shift, 1) for b in range(3)
                    ]
                    for b in range(2):
                        cell = jnp.where(lane < half - shift, rolled[b], rolled[b + 1])
                        patch[c, b, here, :] = cell
                        cells.append(cell)
                lefts = []
                for m in range(modes):
                    waves = []
                    for b in range(2):
                        pr = probe[0, m, here, b * half : (b + 1) * half]
                        pi = probe[1, m, here, b * half : (b + 1) * half]
                        waves.append((pr * cells[b] - pi * cells[2 + b], pr * cells[2 + b] + pi * cells[b]))
                    (ra, ia), (rb, ib) = waves
                    lefts.append((jnp.concatenate([ra + rb, ia + ib], axis=1), jnp.concatenate([ra - rb, ia - ib], axis=1)))
                spectra.append(lefts)
            for parity in range(2):
                stacked = jnp.concatenate([spectra[part][m][parity] for m in range(modes) for part in range(2)], axis=0)
                high, low = split(stacked)
                out = mul(jnp.concatenate([high, low, high], axis=1), jnp.concatenate([tables[parity, 0], tables[parity, 0], tables[parity, 1]], axis=0))
                for m in range(modes):
                    a = out[(2 * m) * CHUNK : (2 * m + 1) * CHUNK]
                    b = out[(2 * m + 1) * CHUNK : (2 * m + 2) * CHUNK]
                    for row_parity, value in enumerate((a + b, a - b)):
                        vh, vl = split(value)
                        for c in range(2):
                            at = slice(c * half + chunk * CHUNK, c * half + (chunk + 1) * CHUNK)
                            to = slice(parity * half, (parity + 1) * half)
                            rows_high[m, row_parity, at, to] = vh[:, c * half : (c + 1) * half]
                            rows_low[m, row_parity, at, to] = vl[:, c * half : (c + 1) * half]

        def row_transform(table, parity):
            for m in range(modes):
                high = rows_high[m, parity]
                low = rows_low[m, parity]
                freq[m, parity] = mul(
                    jnp.concatenate([tables[table + parity, 0], tables[table + parity, 1], tables[table + parity, 0]], axis=1),
                    jnp.concatenate([high, high, low], axis=0),
                )

        def apply_factor(parity):
            for chunk in range(half // CHUNK):
                real = slice(chunk * CHUNK, (chunk + 1) * CHUNK)
                imag = slice(half + chunk * CHUNK, half + (chunk + 1) * CHUNK)
                values = [(freq[m, parity, real, :], freq[m, parity, imag, :]) for m in range(modes)]
                power = sum(re * re + im * im for re, im in values)
                factor = 1.0 - root[slot, parity, real, :] * lax.rsqrt(jnp.maximum(power, FLOOR * FLOOR))
                for m in range(modes):
                    for at, value in zip((real, imag), values[m]):
                        vh, vl = split(value * factor)
                        rows_high[m, parity, at, :] = vh
                        rows_low[m, parity, at, :] = vl

        row_transform(2, 0)
        row_transform(2, 1)
        apply_factor(0)
        row_transform(4, 0)
        apply_factor(1)
        row_transform(4, 1)

        for chunk in range(half // CHUNK):
            real = slice(chunk * CHUNK, (chunk + 1) * CHUNK)
            imag = slice(half + chunk * CHUNK, half + (chunk + 1) * CHUNK)
            backs = []
            for q in range(2):
                cols = slice(q * half, (q + 1) * half)
                pieces = []
                for m in range(modes):
                    even = jnp.concatenate([freq[m, 0, real, cols], freq[m, 0, imag, cols]], axis=1)
                    odd = jnp.concatenate([freq[m, 1, real, cols], freq[m, 1, imag, cols]], axis=1)
                    pieces += [even + odd, even - odd]
                high, low = split(jnp.concatenate(pieces, axis=0))
                backs.append(mul(jnp.concatenate([high, low, high], axis=1), jnp.concatenate([tables[6 + q, 0], tables[6 + q, 0], tables[6 + q, 1]], axis=0)))
            halves = (backs[0] + backs[1], backs[0] - backs[1])
            for part in range(2):
                rows = part * half + chunk * CHUNK
                here = slice(rows, rows + CHUNK)
                total = [[0.0, 0.0], [0.0, 0.0]]
                for b in range(2):
                    xr = patch[0, b, here, :]
                    xi = patch[1, b, here, :]
                    for m in range(modes):
                        at = (2 * m + part) * CHUNK
                        br = halves[b][at : at + CHUNK, :half]
                        bi = halves[b][at : at + CHUNK, half:]
                        pr = probe[0, m, here, b * half : (b + 1) * half]
                        pi = probe[1, m, here, b * half : (b + 1) * half]
                        total[0][b] += pr * br + pi * bi
                        total[1][b] += pr * bi - pi * br
                        sums[pl.ds(((b * 2 + 0) * modes + m) * length + rows, CHUNK), :] += xr * br + xi * bi
                        sums[pl.ds(((b * 2 + 1) * modes + m) * length + rows, CHUNK), :] += xr * bi - xi * br
                for c in range(2):
                    ra = pltpu.roll(total[c][0], fore_shift, 1)
                    rb = pltpu.roll(total[c][1], fore_shift, 1)
                    beyond = lane >= shift
                    zero = jnp.zeros_like(ra)
                    placed = (jnp.where(beyond, ra, zero), jnp.where(beyond, rb, ra), jnp.where(beyond, zero, rb))
                    for b in range(3):
                        grid[c, block + b, pl.ds(row0 + rows, CHUNK), :] += placed[b]
        return carry

    lax.fori_loop(0, scalars[0], slot_step, 0)

    kept, rows, _ = probe_keep.shape
    code = own_code(digit_groups())

    def place_piece(place, carry):
        for first, target in ((0, probe_keep), (kept, probe_sent)):
            piece = (place + first) ^ code
            target[place] = sums[pl.ds(pl.multiple_of(piece * rows, rows), rows), :]
        return carry

    lax.fori_loop(0, kept, place_piece, 0)
    inner_side_out[...] = grid[:, inner]
    outer_side_out[...] = grid[:, outer]
    for b in range(2):
        grad_mid[:, :, b * half : (b + 1) * half] = grid[:, 1 + b]


def rows_kernel(grad_mid, inner_side, outer_side, _, core_out, chip_out, inner_grad):
    margin, length = core_out.shape[1], inner_grad.shape[1]
    near, far = (pl.ds(start, margin) for start in near_and_far(margin + length))
    for side, start in zip((inner_side, outer_side), inner_and_outer()):
        cols = pl.ds(start, LANES)
        for target, rows in ((core_out, near), (chip_out, far), (inner_grad, slice(margin, margin + length))):
            target[:, :, cols] = grad_mid[:, rows, cols] + side[:, rows, :]


def columns_kernel(inner_grad, core_in, chip_in, grad):
    near, far = (pl.ds(start, LANES) for start in near_and_far(LANES))
    grad[:, near, :] = inner_grad[:, near, :] + core_in[...]
    grad[:, far, :] = inner_grad[:, far, :] + chip_in[...]


def after_kernel(_, *refs):
    join_pieces(refs[:-1], refs[-1])


def join_pieces(pieces, joined):
    count = pieces[0].shape[0]
    for i, piece in enumerate(pieces):
        joined[i * count : (i + 1) * count] = piece[...]


def join_kernel(first, *refs):
    source, out, sems = refs[0], refs[-2], refs[-1]
    kept, rows, _ = source.shape
    _, modes, length, _ = out.shape
    code = own_code(digit_groups())
    each = length // rows
    copies = []
    for place in range(kept):
        piece = (place + first) ^ code
        row = pl.multiple_of(piece % each * rows, rows)
        m = piece // each % modes
        c = piece // (each * modes) % 2
        b = pl.multiple_of(piece // (each * modes * 2) * LANES, LANES)
        copies.append(
            pltpu.make_async_copy(source.at[place], out.at[c, m, pl.ds(row, rows), pl.ds(b, LANES)], sems.at[place])
        )
    for copy in copies:
        copy.start()
    for copy in copies:
        copy.wait()


def exchanged(value, axis, mask):
    return lax.ppermute(value, axis, [(i, i ^ mask) for i in range(lax.axis_size(axis))])


def digit_groups():
    groups = [("ty", [1])]
    bits = [1 << i for i in range(1, lax.axis_size("ty").bit_length() - 1)]
    groups += [("ty", bits[i : i + 2]) for i in range(0, len(bits), 2)]
    return groups + [("tx", [1])]


def masks(bits):
    return [sum(bit for i, bit in enumerate(reversed(bits)) if j >> i & 1) for j in range(1 << len(bits))]


def own_code(groups):
    code = 0
    for axis, bits in groups:
        index = lax.axis_index(axis)
        for bit in bits:
            code = code * 2 + (index // bit) % 2
    return code


def pair_partner(index, kind):
    return index ^ 1 if kind == "inner" else index + 1 if index % 2 else index - 1


def paired(value, axis, kind):
    count = lax.axis_size(axis)
    pairs = [(i, pair_partner(i, kind)) for i in range(count)]
    return lax.ppermute(value, axis, [(i, j) for i, j in pairs if 0 <= j < count])


def add_kernel(scale, own, *refs):
    others, out = refs[:-1], refs[-1]
    count = out.shape[0]
    total = own[:count]
    for other in others:
        total += other[...]
    out[...] = total * scale


def added(own, others, scale=1.0, weight=0):
    out = jax.ShapeDtypeStruct(others[0].shape, jnp.float32)
    (result,) = call(functools.partial(add_kernel, scale), "add", [out], (own, *others), weight=weight)
    return result


def scattered(value, axis, bits):
    places = masks(bits)
    count = value.shape[0] // len(places)
    return [exchanged(value[j * count : (j + 1) * count], axis, places[j]) for j in range(1, len(places))]


def gathered(value, axis, bits):
    return [value] + [exchanged(value, axis, mask) for mask in masks(bits)[1:]]


def call(body, name, out, operands, spaces="", results="", scratch=(), limit=SMALL_LIMIT, weight=0, aliases=None):
    kinds = {"v": pltpu.VMEM, "s": pltpu.SMEM, "h": pltpu.HBM}

    def specs(letters, count):
        return tuple(pl.BlockSpec(memory_space=kinds[x]) for x in letters + "v" * (count - len(letters)))

    moved = sum(math.prod(v.shape) * v.dtype.itemsize for v in tuple(operands) + tuple(out))
    return pl.pallas_call(
        body,
        out_shape=tuple(out),
        in_specs=specs(spaces, len(operands)),
        out_specs=specs(results, len(out)),
        scratch_shapes=list(scratch),
        input_output_aliases=aliases or {},
        compiler_params=pltpu.CompilerParams(vmem_limit_bytes=limit),
        cost_estimate=pl.CostEstimate(flops=weight, bytes_accessed=moved, transcendentals=0),
        name=name,
    )(*operands)


def shards(object_field, probe_modes, intensities, offsets, counts):
    length = object_field.shape[1]
    modes, pattern = probe_modes.shape[1:3]
    margin = pattern // 2
    half = LANES
    devices = lax.axis_size("ty") * lax.axis_size("tx")
    groups = digit_groups()
    f32, bf16 = jnp.float32, jnp.bfloat16
    slots = intensities.shape[2]
    tables = jnp.asarray(fourier_tables(pattern))

    def shape(*sizes):
        return jax.ShapeDtypeStruct(sizes, f32)

    tile, rows_shape = shape(2, length, length), shape(2, margin, length)
    side, tall_side, corner = shape(2, length, margin), shape(2, length + 2 * margin, margin), shape(2, margin, margin)
    core_tile = paired(object_field, "ty", "inner")
    (leaving,) = call(chip_edges_kernel, "chip_edges", [rows_shape], (object_field,), "h", scratch=(pltpu.SemaphoreType.DMA,))
    center, inner_side, outer_side = call(
        edges_kernel, "edges", [tile, side, side], (object_field, leaving), "hh", scratch=(pltpu.SemaphoreType.DMA((3,)),), weight=AROUND
    )
    chip_rows = leaving
    chip_rows = paired(chip_rows, "ty", "outer")
    inner_side = paired(inner_side, "tx", "inner")
    outer_side = paired(outer_side, "tx", "outer")
    (root,) = call(
        root_kernel,
        "root",
        [shape(slots, 2, half, pattern)],
        (intensities[0, 0],),
        scratch=(pltpu.VMEM((slots, 2, pattern, half), f32),),
        weight=AROUND,
    )
    (scalars,) = call(
        places_kernel, "places", [jax.ShapeDtypeStruct((1 + 2 * slots,), jnp.int32)], (counts.T, offsets[0, 0].T), "ss", "s", weight=AROUND
    )
    inner_corner, outer_corner = call(corners_kernel, "corners", [corner, corner], (chip_rows, root, scalars), "vhh")
    inner_corner = paired(inner_corner, "tx", "inner")
    outer_corner = paired(outer_corner, "tx", "outer")
    inner_near, outer_near = call(near_kernel, "near", [corner, corner], (inner_side, outer_side))
    inner_near = paired(inner_near, "ty", "inner")
    outer_near = paired(outer_near, "ty", "inner")
    (far_rows,) = call(far_kernel, "far", [shape(2, 4, margin, half)], (chip_rows, inner_corner, outer_corner), weight=AHEAD)
    pieces = 1 << sum(len(bits) for _, bits in groups)
    rows = 2 * 2 * modes * pattern // pieces
    kept = shape(pieces // 2, rows, half)
    probe_sent, value, inner_side, outer_side, grad_mid = call(
        slots_kernel,
        "slots",
        [kept, kept, tall_side, tall_side, shape(2, length + 2 * margin, length)],
        (
            scalars, center, core_tile, far_rows, inner_side, outer_side, inner_near, outer_near,
            probe_modes, root, tables,
        ),
        "s",
        scratch=(
            pltpu.VMEM((2, 4, length + 2 * margin, half), f32),
            pltpu.VMEM((2, 4, length + 2 * margin, half), f32),
            pltpu.VMEM((2, 2, pattern, half), f32),
            pltpu.VMEM((modes, 2, pattern, pattern), bf16),
            pltpu.VMEM((modes, 2, pattern, pattern), bf16),
            pltpu.VMEM((modes, 2, pattern, pattern), f32),
            pltpu.VMEM((2 * 2 * modes * pattern, half), f32),
        ),
        limit=VMEM_LIMIT,
    )

    value = added(value, [paired(probe_sent, "ty", "inner")], weight=HEAVY)
    inner_side = paired(inner_side, "tx", "inner")
    outer_side = paired(outer_side, "tx", "outer")
    for group in groups[1:-1]:
        value = added(value, scattered(value, *group))
    value = added(value, scattered(value, *groups[-1]), scale=1.0 / devices)
    core_rows, chip_rows, inner_grad = call(
        rows_kernel,
        "rows",
        [rows_shape, rows_shape, tile],
        (grad_mid, inner_side, outer_side, value),
        "vvvh",
        weight=HEAVY,
    )
    chip_rows = paired(chip_rows, "ty", "outer")
    core_rows = paired(core_rows, "ty", "inner")
    for i in range(1, lax.axis_size("tx").bit_length() - 1):
        value = added(value, [exchanged(value, "tx", 1 << i)], weight=4000000000)
    for i in range(len(groups) - 1, 0, -1):
        parts = gathered(value, *groups[i])
        joined = shape(len(parts) * value.shape[0], rows, half)
        arrived = chip_rows if i == len(groups) - 1 else core_rows
        (value,) = call(after_kernel, "after", [joined], (arrived, *parts), "h", weight=4000000000)
    (object_grad,) = call(columns_kernel, "columns", [tile], (inner_grad, core_rows, chip_rows))
    other = paired(value, "ty", "inner")
    sems = (pltpu.SemaphoreType.DMA((pieces // 2,)),)
    (probe_grad,) = call(
        functools.partial(join_kernel, 0), "join", [shape(*probe_modes.shape)], (value,), "v", "h", sems, weight=AROUND
    )
    (probe_grad,) = call(
        functools.partial(join_kernel, pieces // 2),
        "join_rest",
        [shape(*probe_modes.shape)],
        (other, probe_grad),
        "vh",
        "h",
        sems,
        aliases={1: 0},
    )
    return (object_grad, probe_grad)


def solution(mesh):
    placed = (
        P(None, "ty", "tx"),
        P(),
        P("ty", "tx", None, None, None),
        P("ty", "tx", None, None),
        P(),
    )
    return jax.shard_map(
        shards, mesh=mesh, in_specs=placed, out_specs=(P(None, "ty", "tx"), P()), check_vma=False
    )
```

```python
import functools
import math

import jax
import jax.numpy as jnp
import ml_dtypes
import numpy as np
from jax import lax
from jax.experimental import pallas as pl
from jax.experimental.pallas import tpu as pltpu
from jax.sharding import PartitionSpec as P

FLOOR = 0.5
LANES = 128
CHUNK = 64
HEAVY = 0
AHEAD = 4_000_000_000
AROUND = 2_000_000_000
VMEM_LIMIT = 28 * 1024 * 1024
SMALL_LIMIT = 8 * 1024 * 1024


def split_table(table):
    high = table.astype(ml_dtypes.bfloat16)
    low = (table - high.astype(np.float64)).astype(ml_dtypes.bfloat16)
    return high, low


def complex_block(matrix):
    return np.block([[matrix.real, matrix.imag], [-matrix.imag, matrix.real]])


@functools.lru_cache(maxsize=None)
def fourier_tables(pattern):
    half = pattern // 2
    n = np.arange(half)
    tables = []
    for parity in (0, 1):
        k = 2 * np.arange(half) + parity
        tables.append(np.exp(-2j * np.pi * ((n[:, None] * k[None, :]) % pattern) / pattern) / math.sqrt(pattern))
    forward = [complex_block(t) for t in tables]
    inverse = [complex_block(np.conj(t).T) for t in tables]
    every = forward + [t.T for t in forward] + [t.T for t in inverse] + inverse
    return np.stack([np.stack(split_table(t)) for t in every])


def split(value):
    high = value.astype(jnp.bfloat16)
    low = (value - high.astype(jnp.float32)).astype(jnp.bfloat16)
    return high, low


def mul(a, b):
    return jnp.dot(a, b, preferred_element_type=jnp.float32)


def near_and_far(unit):
    odd = lax.axis_index("ty") % 2
    return pl.multiple_of((1 - odd) * unit, LANES), pl.multiple_of(odd * unit, LANES)


def inner_and_outer():
    odd = lax.axis_index("tx") % 2
    return pl.multiple_of((1 - odd) * LANES, LANES), pl.multiple_of(odd * LANES, LANES)


def chip_edges_kernel(field, chip_rows, sem):
    _, far = near_and_far(LANES)
    copy = pltpu.make_async_copy(field.at[:, pl.ds(far, LANES), :], chip_rows, sem)
    copy.start()
    copy.wait()


def edges_kernel(field, _, center, inner_side, outer_side, sems):
    inner, outer = inner_and_outer()
    moves = (
        (field.at[:, :, pl.ds(inner, LANES)], inner_side),
        (field.at[:, :, pl.ds(outer, LANES)], outer_side),
        (field, center),
    )
    copies = [pltpu.make_async_copy(source, target, sems.at[i]) for i, (source, target) in enumerate(moves)]
    for copy in copies:
        copy.start()
    for copy in copies:
        copy.wait()


def near_kernel(inner_side, outer_side, inner_near, outer_near):
    near, _ = near_and_far(LANES)
    inner_near[...] = inner_side[:, pl.ds(near, LANES), :]
    outer_near[...] = outer_side[:, pl.ds(near, LANES), :]


def far_kernel(chip_rows, inner_corner, outer_corner, far_rows):
    inner = (1 - lax.axis_index("tx") % 2) * 3
    for b in range(2):
        far_rows[:, 1 + b] = chip_rows[:, :, b * LANES : (b + 1) * LANES]
    far_rows[:, inner] = inner_corner[...]
    far_rows[:, 3 - inner] = outer_corner[...]


def corners_kernel(chip_rows, _, __, inner_corner, outer_corner):
    for target, start in zip((inner_corner, outer_corner), inner_and_outer()):
        target[...] = chip_rows[:, :, pl.ds(start, LANES)]


def root_kernel(measured, root, halves):
    pattern = measured.shape[2]
    source = lax.broadcasted_iota(jnp.int32, (pattern, pattern), 0)
    place = lax.broadcasted_iota(jnp.int32, (pattern, pattern), 1)
    half = pattern // 2
    wanted = jnp.where(place < half, 2 * place, 2 * (place - half) + 1)
    order = jnp.where(source == wanted, 1.0, 0.0).astype(jnp.bfloat16)
    for slot in range(measured.shape[0]):
        for b in range(2):
            halves[slot, b] = jnp.sqrt(measured[slot, :, b * LANES : (b + 1) * LANES])
        for parity in range(2):
            rows = pl.ds(parity, LANES, stride=2)
            high, low = split(jnp.concatenate([halves[slot, 0, rows, :], halves[slot, 1, rows, :]], axis=1))
            root[slot, parity] = mul(high, order) + mul(low, order)


def places_kernel(counts, spots, scalars):
    scalars[0] = counts[lax.axis_index("tx"), lax.axis_index("ty")]
    for slot in range(spots.shape[1]):
        for axis in range(2):
            scalars[1 + 2 * slot + axis] = spots[axis, slot]


def slots_kernel(
    scalars, center, core_tile, far_rows, inner_side, outer_side, inner_near, outer_near, probe, root, tables,
    sums, inner_side_out, outer_side_out, grad_mid,
    pad, grid, patch, rows_high, rows_low, freq,
):
    half = LANES
    modes = probe.shape[1]
    length = center.shape[1]
    margin = far_rows.shape[2]
    near, far = near_and_far(margin + length)
    near, far, own = pl.ds(near, margin), pl.ds(far, margin), pl.ds(margin, length)
    core_half = pl.ds(pl.multiple_of(lax.axis_index("ty") % 2 * half, half), half)
    inner = (1 - lax.axis_index("tx") % 2) * 3
    outer = 3 - inner

    for b in range(2):
        cols = slice(b * half, (b + 1) * half)
        pad[:, 1 + b, margin : margin + length, :] = center[:, :, cols]
        pad[:, 1 + b, near, :] = core_tile[:, core_half, cols]
    pad[:, inner, own, :] = inner_side[...]
    pad[:, outer, own, :] = outer_side[...]
    pad[:, inner, near, :] = inner_near[...]
    pad[:, outer, near, :] = outer_near[...]
    pad[:, :, far, :] = far_rows[...]
    grid[...] = jnp.zeros_like(grid)
    code = own_code(digit_groups())
    piece_rows = sums.shape[1]
    sums[...] = jnp.zeros_like(sums)
    lane = lax.broadcasted_iota(jnp.int32, (CHUNK, half), 1)

    def slot_step(slot, carry):
        row0 = scalars[1 + 2 * slot]
        col0 = scalars[2 + 2 * slot]
        block = jnp.minimum(col0 // half, 1)
        shift = col0 - block * half
        back_shift = lax.rem(half - shift, half)
        fore_shift = lax.rem(shift, half)

        for chunk in range(half // CHUNK):
            spectra = []
            for part in range(2):
                rows = part * half + chunk * CHUNK
                here = slice(rows, rows + CHUNK)
                cells = []
                for c in range(2):
                    rolled = [
                        pltpu.roll(pad[c, block + b, pl.ds(row0 + rows, CHUNK), :], back_shift, 1) for b in range(3)
                    ]
                    for b in range(2):
                        cell = jnp.where(lane < half - shift, rolled[b], rolled[b + 1])
                        patch[c, b, here, :] = cell
                        cells.append(cell)
                lefts = []
                for m in range(modes):
                    waves = []
                    for b in range(2):
                        pr = probe[0, m, here, b * half : (b + 1) * half]
                        pi = probe[1, m, here, b * half : (b + 1) * half]
                        waves.append((pr * cells[b] - pi * cells[2 + b], pr * cells[2 + b] + pi * cells[b]))
                    (ra, ia), (rb, ib) = waves
                    lefts.append((jnp.concatenate([ra + rb, ia + ib], axis=1), jnp.concatenate([ra - rb, ia - ib], axis=1)))
                spectra.append(lefts)
            for parity in range(2):
                stacked = jnp.concatenate([spectra[part][m][parity] for m in range(modes) for part in range(2)], axis=0)
                high, low = split(stacked)
                out = mul(jnp.concatenate([high, low, high], axis=1), jnp.concatenate([tables[parity, 0], tables[parity, 0], tables[parity, 1]], axis=0))
                for m in range(modes):
                    a = out[(2 * m) * CHUNK : (2 * m + 1) * CHUNK]
                    b = out[(2 * m + 1) * CHUNK : (2 * m + 2) * CHUNK]
                    for row_parity, value in enumerate((a + b, a - b)):
                        vh, vl = split(value)
                        for c in range(2):
                            at = slice(c * half + chunk * CHUNK, c * half + (chunk + 1) * CHUNK)
                            to = slice(parity * half, (parity + 1) * half)
                            rows_high[m, row_parity, at, to] = vh[:, c * half : (c + 1) * half]
                            rows_low[m, row_parity, at, to] = vl[:, c * half : (c + 1) * half]

        def row_transform(table, parity):
            for m in range(modes):
                high = rows_high[m, parity]
                low = rows_low[m, parity]
                freq[m, parity] = mul(
                    jnp.concatenate([tables[table + parity, 0], tables[table + parity, 1], tables[table + parity, 0]], axis=1),
                    jnp.concatenate([high, high, low], axis=0),
                )

        def apply_factor(parity):
            for chunk in range(half // CHUNK):
                real = slice(chunk * CHUNK, (chunk + 1) * CHUNK)
                imag = slice(half + chunk * CHUNK, half + (chunk + 1) * CHUNK)
                values = [(freq[m, parity, real, :], freq[m, parity, imag, :]) for m in range(modes)]
                power = sum(re * re + im * im for re, im in values)
                factor = 1.0 - root[slot, parity, real, :] * lax.rsqrt(jnp.maximum(power, FLOOR * FLOOR))
                for m in range(modes):
                    for at, value in zip((real, imag), values[m]):
                        vh, vl = split(value * factor)
                        rows_high[m, parity, at, :] = vh
                        rows_low[m, parity, at, :] = vl

        row_transform(2, 0)
        row_transform(2, 1)
        apply_factor(0)
        row_transform(4, 0)
        apply_factor(1)
        row_transform(4, 1)

        for chunk in range(half // CHUNK):
            real = slice(chunk * CHUNK, (chunk + 1) * CHUNK)
            imag = slice(half + chunk * CHUNK, half + (chunk + 1) * CHUNK)
            backs = []
            for q in range(2):
                cols = slice(q * half, (q + 1) * half)
                pieces = []
                for m in range(modes):
                    even = jnp.concatenate([freq[m, 0, real, cols], freq[m, 0, imag, cols]], axis=1)
                    odd = jnp.concatenate([freq[m, 1, real, cols], freq[m, 1, imag, cols]], axis=1)
                    pieces += [even + odd, even - odd]
                high, low = split(jnp.concatenate(pieces, axis=0))
                backs.append(mul(jnp.concatenate([high, low, high], axis=1), jnp.concatenate([tables[6 + q, 0], tables[6 + q, 0], tables[6 + q, 1]], axis=0)))
            halves = (backs[0] + backs[1], backs[0] - backs[1])
            for part in range(2):
                rows = part * half + chunk * CHUNK
                here = slice(rows, rows + CHUNK)
                total = [[0.0, 0.0], [0.0, 0.0]]
                for b in range(2):
                    xr = patch[0, b, here, :]
                    xi = patch[1, b, here, :]
                    for m in range(modes):
                        at = (2 * m + part) * CHUNK
                        br = halves[b][at : at + CHUNK, :half]
                        bi = halves[b][at : at + CHUNK, half:]
                        pr = probe[0, m, here, b * half : (b + 1) * half]
                        pi = probe[1, m, here, b * half : (b + 1) * half]
                        total[0][b] += pr * br + pi * bi
                        total[1][b] += pr * bi - pi * br
                        sums[((((b * 2 + 0) * modes + m) * length + rows) // piece_rows) ^ code, pl.ds(rows % piece_rows, CHUNK), :] += xr * br + xi * bi
                        sums[((((b * 2 + 1) * modes + m) * length + rows) // piece_rows) ^ code, pl.ds(rows % piece_rows, CHUNK), :] += xr * bi - xi * br
                for c in range(2):
                    ra = pltpu.roll(total[c][0], fore_shift, 1)
                    rb = pltpu.roll(total[c][1], fore_shift, 1)
                    beyond = lane >= shift
                    zero = jnp.zeros_like(ra)
                    placed = (jnp.where(beyond, ra, zero), jnp.where(beyond, rb, ra), jnp.where(beyond, zero, rb))
                    for b in range(3):
                        grid[c, block + b, pl.ds(row0 + rows, CHUNK), :] += placed[b]
        return carry

    lax.fori_loop(0, scalars[0], slot_step, 0)

    inner_side_out[...] = grid[:, inner]
    outer_side_out[...] = grid[:, outer]
    for b in range(2):
        grad_mid[:, :, b * half : (b + 1) * half] = grid[:, 1 + b]


def rows_kernel(grad_mid, inner_side, outer_side, _, core_out, chip_out, inner_grad):
    margin, length = core_out.shape[1], inner_grad.shape[1]
    near, far = (pl.ds(start, margin) for start in near_and_far(margin + length))
    for side, start in zip((inner_side, outer_side), inner_and_outer()):
        cols = pl.ds(start, LANES)
        for target, rows in ((core_out, near), (chip_out, far), (inner_grad, slice(margin, margin + length))):
            target[:, :, cols] = grad_mid[:, rows, cols] + side[:, rows, :]


def columns_kernel(inner_grad, core_in, chip_in, grad):
    near, far = (pl.ds(start, LANES) for start in near_and_far(LANES))
    grad[:, near, :] = inner_grad[:, near, :] + core_in[...]
    grad[:, far, :] = inner_grad[:, far, :] + chip_in[...]


def after_kernel(_, *refs):
    join_pieces(refs[:-1], refs[-1])


def join_pieces(pieces, joined):
    count = pieces[0].shape[0]
    for i, piece in enumerate(pieces):
        joined[i * count : (i + 1) * count] = piece[...]


def join_kernel(first, *refs):
    source, out, sems = refs[0], refs[-2], refs[-1]
    kept, rows, _ = source.shape
    _, modes, length, _ = out.shape
    code = own_code(digit_groups())
    each = length // rows
    copies = []
    for place in range(kept):
        piece = (place + first) ^ code
        row = pl.multiple_of(piece % each * rows, rows)
        m = piece // each % modes
        c = piece // (each * modes) % 2
        b = pl.multiple_of(piece // (each * modes * 2) * LANES, LANES)
        copies.append(
            pltpu.make_async_copy(source.at[place], out.at[c, m, pl.ds(row, rows), pl.ds(b, LANES)], sems.at[place])
        )
    for copy in copies:
        copy.start()
    for copy in copies:
        copy.wait()


def exchanged(value, axis, mask):
    return lax.ppermute(value, axis, [(i, i ^ mask) for i in range(lax.axis_size(axis))])


def digit_groups():
    groups = [("ty", [1])]
    bits = [1 << i for i in range(1, lax.axis_size("ty").bit_length() - 1)]
    groups += [("ty", bits[i : i + 2]) for i in range(0, len(bits), 2)]
    return groups + [("tx", [1])]


def masks(bits):
    return [sum(bit for i, bit in enumerate(reversed(bits)) if j >> i & 1) for j in range(1 << len(bits))]


def own_code(groups):
    code = 0
    for axis, bits in groups:
        index = lax.axis_index(axis)
        for bit in bits:
            code = code * 2 + (index // bit) % 2
    return code


def pair_partner(index, kind):
    return index ^ 1 if kind == "inner" else index + 1 if index % 2 else index - 1


def paired(value, axis, kind):
    count = lax.axis_size(axis)
    pairs = [(i, pair_partner(i, kind)) for i in range(count)]
    return lax.ppermute(value, axis, [(i, j) for i, j in pairs if 0 <= j < count])


def add_kernel(scale, own, *refs):
    others, out = refs[:-1], refs[-1]
    count = out.shape[0]
    total = own[:count]
    for other in others:
        total += other[...]
    out[...] = total * scale


def added(own, others, scale=1.0, weight=0):
    out = jax.ShapeDtypeStruct(others[0].shape, jnp.float32)
    (result,) = call(functools.partial(add_kernel, scale), "add", [out], (own, *others), weight=weight)
    return result


def scattered(value, axis, bits):
    places = masks(bits)
    count = value.shape[0] // len(places)
    return [exchanged(value[j * count : (j + 1) * count], axis, places[j]) for j in range(1, len(places))]


def gathered(value, axis, bits):
    return [value] + [exchanged(value, axis, mask) for mask in masks(bits)[1:]]


def call(body, name, out, operands, spaces="", results="", scratch=(), limit=SMALL_LIMIT, weight=0, aliases=None):
    kinds = {"v": pltpu.VMEM, "s": pltpu.SMEM, "h": pltpu.HBM}

    def specs(letters, count):
        return tuple(pl.BlockSpec(memory_space=kinds[x]) for x in letters + "v" * (count - len(letters)))

    moved = sum(math.prod(v.shape) * v.dtype.itemsize for v in tuple(operands) + tuple(out))
    return pl.pallas_call(
        body,
        out_shape=tuple(out),
        in_specs=specs(spaces, len(operands)),
        out_specs=specs(results, len(out)),
        scratch_shapes=list(scratch),
        input_output_aliases=aliases or {},
        compiler_params=pltpu.CompilerParams(vmem_limit_bytes=limit),
        cost_estimate=pl.CostEstimate(flops=weight, bytes_accessed=moved, transcendentals=0),
        name=name,
    )(*operands)


def shards(object_field, probe_modes, intensities, offsets, counts):
    length = object_field.shape[1]
    modes, pattern = probe_modes.shape[1:3]
    margin = pattern // 2
    half = LANES
    devices = lax.axis_size("ty") * lax.axis_size("tx")
    groups = digit_groups()
    f32, bf16 = jnp.float32, jnp.bfloat16
    slots = intensities.shape[2]
    tables = jnp.asarray(fourier_tables(pattern))

    def shape(*sizes):
        return jax.ShapeDtypeStruct(sizes, f32)

    tile, rows_shape = shape(2, length, length), shape(2, margin, length)
    side, tall_side, corner = shape(2, length, margin), shape(2, length + 2 * margin, margin), shape(2, margin, margin)
    core_tile = paired(object_field, "ty", "inner")
    (leaving,) = call(chip_edges_kernel, "chip_edges", [rows_shape], (object_field,), "h", scratch=(pltpu.SemaphoreType.DMA,))
    center, inner_side, outer_side = call(
        edges_kernel, "edges", [tile, side, side], (object_field, leaving), "hh", scratch=(pltpu.SemaphoreType.DMA((3,)),), weight=AROUND
    )
    chip_rows = leaving
    chip_rows = paired(chip_rows, "ty", "outer")
    inner_side = paired(inner_side, "tx", "inner")
    outer_side = paired(outer_side, "tx", "outer")
    (root,) = call(
        root_kernel,
        "root",
        [shape(slots, 2, half, pattern)],
        (intensities[0, 0],),
        scratch=(pltpu.VMEM((slots, 2, pattern, half), f32),),
        weight=AROUND,
    )
    (scalars,) = call(
        places_kernel, "places", [jax.ShapeDtypeStruct((1 + 2 * slots,), jnp.int32)], (counts.T, offsets[0, 0].T), "ss", "s", weight=AROUND
    )
    inner_corner, outer_corner = call(corners_kernel, "corners", [corner, corner], (chip_rows, root, scalars), "vhh")
    inner_corner = paired(inner_corner, "tx", "inner")
    outer_corner = paired(outer_corner, "tx", "outer")
    inner_near, outer_near = call(near_kernel, "near", [corner, corner], (inner_side, outer_side))
    inner_near = paired(inner_near, "ty", "inner")
    outer_near = paired(outer_near, "ty", "inner")
    (far_rows,) = call(far_kernel, "far", [shape(2, 4, margin, half)], (chip_rows, inner_corner, outer_corner), weight=AHEAD)
    pieces = 1 << sum(len(bits) for _, bits in groups)
    rows = 2 * 2 * modes * pattern // pieces
    value, inner_side, outer_side, grad_mid = call(
        slots_kernel,
        "slots",
        [shape(pieces, rows, half), tall_side, tall_side, shape(2, length + 2 * margin, length)],
        (
            scalars, center, core_tile, far_rows, inner_side, outer_side, inner_near, outer_near,
            probe_modes, root, tables,
        ),
        "s",
        scratch=(
            pltpu.VMEM((2, 4, length + 2 * margin, half), f32),
            pltpu.VMEM((2, 4, length + 2 * margin, half), f32),
            pltpu.VMEM((2, 2, pattern, half), f32),
            pltpu.VMEM((modes, 2, pattern, pattern), bf16),
            pltpu.VMEM((modes, 2, pattern, pattern), bf16),
            pltpu.VMEM((modes, 2, pattern, pattern), f32),
        ),
        limit=VMEM_LIMIT,
    )

    value = added(value, [paired(value[pieces // 2 :], "ty", "inner")], weight=HEAVY)
    inner_side = paired(inner_side, "tx", "inner")
    outer_side = paired(outer_side, "tx", "outer")
    for group in groups[1:-1]:
        value = added(value, scattered(value, *group))
    value = added(value, scattered(value, *groups[-1]), scale=1.0 / devices)
    core_rows, chip_rows, inner_grad = call(
        rows_kernel,
        "rows",
        [rows_shape, rows_shape, tile],
        (grad_mid, inner_side, outer_side, value),
        "vvvh",
        weight=HEAVY,
    )
    chip_rows = paired(chip_rows, "ty", "outer")
    core_rows = paired(core_rows, "ty", "inner")
    for i in range(1, lax.axis_size("tx").bit_length() - 1):
        value = added(value, [exchanged(value, "tx", 1 << i)], weight=4000000000)
    for i in range(len(groups) - 1, 0, -1):
        parts = gathered(value, *groups[i])
        joined = shape(len(parts) * value.shape[0], rows, half)
        arrived = chip_rows if i == len(groups) - 1 else core_rows
        (value,) = call(after_kernel, "after", [joined], (arrived, *parts), "h", weight=4000000000)
    (object_grad,) = call(columns_kernel, "columns", [tile], (inner_grad, core_rows, chip_rows))
    other = paired(value, "ty", "inner")
    sems = (pltpu.SemaphoreType.DMA((pieces // 2,)),)
    (probe_grad,) = call(
        functools.partial(join_kernel, 0), "join", [shape(*probe_modes.shape)], (value,), "v", "h", sems, weight=AROUND
    )
    (probe_grad,) = call(
        functools.partial(join_kernel, pieces // 2),
        "join_rest",
        [shape(*probe_modes.shape)],
        (other, probe_grad),
        "vh",
        "h",
        sems,
        aliases={1: 0},
    )
    return (object_grad, probe_grad)


def solution(mesh):
    placed = (
        P(None, "ty", "tx"),
        P(),
        P("ty", "tx", None, None, None),
        P("ty", "tx", None, None),
        P(),
    )
    return jax.shard_map(
        shards, mesh=mesh, in_specs=placed, out_specs=(P(None, "ty", "tx"), P()), check_vma=False
    )
```

```python
import functools
import math

import jax
import jax.numpy as jnp
import ml_dtypes
import numpy as np
from jax import lax
from jax.experimental import pallas as pl
from jax.experimental.pallas import tpu as pltpu
from jax.sharding import PartitionSpec as P

FLOOR = 0.5
LANES = 128
CHUNK = 64
HEAVY = 0
AHEAD = 4_000_000_000
AROUND = 2_000_000_000
VMEM_LIMIT = 28 * 1024 * 1024
SMALL_LIMIT = 8 * 1024 * 1024


def split_table(table):
    high = table.astype(ml_dtypes.bfloat16)
    low = (table - high.astype(np.float64)).astype(ml_dtypes.bfloat16)
    return high, low


def complex_block(matrix):
    return np.block([[matrix.real, matrix.imag], [-matrix.imag, matrix.real]])


@functools.lru_cache(maxsize=None)
def fourier_tables(pattern):
    half = pattern // 2
    n = np.arange(half)
    tables = []
    for parity in (0, 1):
        k = 2 * np.arange(half) + parity
        tables.append(np.exp(-2j * np.pi * ((n[:, None] * k[None, :]) % pattern) / pattern) / math.sqrt(pattern))
    forward = [complex_block(t) for t in tables]
    inverse = [complex_block(np.conj(t).T) for t in tables]
    every = forward + [t.T for t in forward] + [t.T for t in inverse] + inverse
    return np.stack([np.stack(split_table(t)) for t in every])


def split(value):
    high = value.astype(jnp.bfloat16)
    low = (value - high.astype(jnp.float32)).astype(jnp.bfloat16)
    return high, low


def mul(a, b):
    return jnp.dot(a, b, preferred_element_type=jnp.float32)


def near_and_far(unit):
    odd = lax.axis_index("ty") % 2
    return pl.multiple_of((1 - odd) * unit, LANES), pl.multiple_of(odd * unit, LANES)


def inner_and_outer():
    odd = lax.axis_index("tx") % 2
    return pl.multiple_of((1 - odd) * LANES, LANES), pl.multiple_of(odd * LANES, LANES)


def chip_edges_kernel(field, chip_rows, sem):
    _, far = near_and_far(LANES)
    copy = pltpu.make_async_copy(field.at[:, pl.ds(far, LANES), :], chip_rows, sem)
    copy.start()
    copy.wait()


def edges_kernel(field, _, center, inner_side, outer_side, sems):
    inner, outer = inner_and_outer()
    moves = (
        (field.at[:, :, pl.ds(inner, LANES)], inner_side),
        (field.at[:, :, pl.ds(outer, LANES)], outer_side),
        (field, center),
    )
    copies = [pltpu.make_async_copy(source, target, sems.at[i]) for i, (source, target) in enumerate(moves)]
    for copy in copies:
        copy.start()
    for copy in copies:
        copy.wait()


def near_kernel(inner_side, outer_side, corners):
    near, _ = near_and_far(LANES)
    corners[0] = inner_side[:, pl.ds(near, LANES), :]
    corners[1] = outer_side[:, pl.ds(near, LANES), :]


def far_kernel(chip_rows, inner_corner, outer_corner, far_rows):
    inner = (1 - lax.axis_index("tx") % 2) * 3
    for b in range(2):
        far_rows[:, 1 + b] = chip_rows[:, :, b * LANES : (b + 1) * LANES]
    far_rows[:, inner] = inner_corner[...]
    far_rows[:, 3 - inner] = outer_corner[...]


def corners_kernel(chip_rows, _, __, inner_corner, outer_corner):
    for target, start in zip((inner_corner, outer_corner), inner_and_outer()):
        target[...] = chip_rows[:, :, pl.ds(start, LANES)]


def root_kernel(measured, root, halves):
    pattern = measured.shape[2]
    source = lax.broadcasted_iota(jnp.int32, (pattern, pattern), 0)
    place = lax.broadcasted_iota(jnp.int32, (pattern, pattern), 1)
    half = pattern // 2
    wanted = jnp.where(place < half, 2 * place, 2 * (place - half) + 1)
    order = jnp.where(source == wanted, 1.0, 0.0).astype(jnp.bfloat16)
    for slot in range(measured.shape[0]):
        for b in range(2):
            halves[slot, b] = jnp.sqrt(measured[slot, :, b * LANES : (b + 1) * LANES])
        for parity in range(2):
            rows = pl.ds(parity, LANES, stride=2)
            high, low = split(jnp.concatenate([halves[slot, 0, rows, :], halves[slot, 1, rows, :]], axis=1))
            root[slot, parity] = mul(high, order) + mul(low, order)


def places_kernel(counts, spots, scalars):
    scalars[0] = counts[lax.axis_index("tx"), lax.axis_index("ty")]
    for slot in range(spots.shape[1]):
        for axis in range(2):
            scalars[1 + 2 * slot + axis] = spots[axis, slot]


def slots_kernel(
    scalars, center, core_tile, far_rows, inner_side, outer_side, near_corners, probe, root, tables,
    sums, inner_side_out, outer_side_out, grad_mid,
    pad, grid, patch, rows_high, rows_low, freq,
):
    half = LANES
    modes = probe.shape[1]
    length = center.shape[1]
    margin = far_rows.shape[2]
    near, far = near_and_far(margin + length)
    near, far, own = pl.ds(near, margin), pl.ds(far, margin), pl.ds(margin, length)
    core_half = pl.ds(pl.multiple_of(lax.axis_index("ty") % 2 * half, half), half)
    inner = (1 - lax.axis_index("tx") % 2) * 3
    outer = 3 - inner

    for b in range(2):
        cols = slice(b * half, (b + 1) * half)
        pad[:, 1 + b, margin : margin + length, :] = center[:, :, cols]
        pad[:, 1 + b, near, :] = core_tile[:, core_half, cols]
    pad[:, inner, own, :] = inner_side[...]
    pad[:, outer, own, :] = outer_side[...]
    pad[:, inner, near, :] = near_corners[0]
    pad[:, outer, near, :] = near_corners[1]
    pad[:, :, far, :] = far_rows[...]
    grid[...] = jnp.zeros_like(grid)
    code = own_code(digit_groups())
    piece_rows = sums.shape[1]
    sums[...] = jnp.zeros_like(sums)
    lane = lax.broadcasted_iota(jnp.int32, (CHUNK, half), 1)

    def slot_step(slot, carry):
        row0 = scalars[1 + 2 * slot]
        col0 = scalars[2 + 2 * slot]
        block = jnp.minimum(col0 // half, 1)
        shift = col0 - block * half
        back_shift = lax.rem(half - shift, half)
        fore_shift = lax.rem(shift, half)

        for chunk in range(half // CHUNK):
            spectra = []
            for part in range(2):
                rows = part * half + chunk * CHUNK
                here = slice(rows, rows + CHUNK)
                cells = []
                for c in range(2):
                    rolled = [
                        pltpu.roll(pad[c, block + b, pl.ds(row0 + rows, CHUNK), :], back_shift, 1) for b in range(3)
                    ]
                    for b in range(2):
                        cell = jnp.where(lane < half - shift, rolled[b], rolled[b + 1])
                        patch[c, b, here, :] = cell
                        cells.append(cell)
                lefts = []
                for m in range(modes):
                    waves = []
                    for b in range(2):
                        pr = probe[0, m, here, b * half : (b + 1) * half]
                        pi = probe[1, m, here, b * half : (b + 1) * half]
                        waves.append((pr * cells[b] - pi * cells[2 + b], pr * cells[2 + b] + pi * cells[b]))
                    (ra, ia), (rb, ib) = waves
                    lefts.append((jnp.concatenate([ra + rb, ia + ib], axis=1), jnp.concatenate([ra - rb, ia - ib], axis=1)))
                spectra.append(lefts)
            for parity in range(2):
                stacked = jnp.concatenate([spectra[part][m][parity] for m in range(modes) for part in range(2)], axis=0)
                high, low = split(stacked)
                out = mul(jnp.concatenate([high, low, high], axis=1), jnp.concatenate([tables[parity, 0], tables[parity, 0], tables[parity, 1]], axis=0))
                for m in range(modes):
                    a = out[(2 * m) * CHUNK : (2 * m + 1) * CHUNK]
                    b = out[(2 * m + 1) * CHUNK : (2 * m + 2) * CHUNK]
                    for row_parity, value in enumerate((a + b, a - b)):
                        vh, vl = split(value)
                        for c in range(2):
                            at = slice(c * half + chunk * CHUNK, c * half + (chunk + 1) * CHUNK)
                            to = slice(parity * half, (parity + 1) * half)
                            rows_high[m, row_parity, at, to] = vh[:, c * half : (c + 1) * half]
                            rows_low[m, row_parity, at, to] = vl[:, c * half : (c + 1) * half]

        def row_transform(table, parity):
            for m in range(modes):
                high = rows_high[m, parity]
                low = rows_low[m, parity]
                freq[m, parity] = mul(
                    jnp.concatenate([tables[table + parity, 0], tables[table + parity, 1], tables[table + parity, 0]], axis=1),
                    jnp.concatenate([high, high, low], axis=0),
                )

        def apply_factor(parity):
            for chunk in range(half // CHUNK):
                real = slice(chunk * CHUNK, (chunk + 1) * CHUNK)
                imag = slice(half + chunk * CHUNK, half + (chunk + 1) * CHUNK)
                values = [(freq[m, parity, real, :], freq[m, parity, imag, :]) for m in range(modes)]
                power = sum(re * re + im * im for re, im in values)
                factor = 1.0 - root[slot, parity, real, :] * lax.rsqrt(jnp.maximum(power, FLOOR * FLOOR))
                for m in range(modes):
                    for at, value in zip((real, imag), values[m]):
                        vh, vl = split(value * factor)
                        rows_high[m, parity, at, :] = vh
                        rows_low[m, parity, at, :] = vl

        row_transform(2, 0)
        row_transform(2, 1)
        apply_factor(0)
        row_transform(4, 0)
        apply_factor(1)
        row_transform(4, 1)

        for chunk in range(half // CHUNK):
            real = slice(chunk * CHUNK, (chunk + 1) * CHUNK)
            imag = slice(half + chunk * CHUNK, half + (chunk + 1) * CHUNK)
            backs = []
            for q in range(2):
                cols = slice(q * half, (q + 1) * half)
                pieces = []
                for m in range(modes):
                    even = jnp.concatenate([freq[m, 0, real, cols], freq[m, 0, imag, cols]], axis=1)
                    odd = jnp.concatenate([freq[m, 1, real, cols], freq[m, 1, imag, cols]], axis=1)
                    pieces += [even + odd, even - odd]
                high, low = split(jnp.concatenate(pieces, axis=0))
                backs.append(mul(jnp.concatenate([high, low, high], axis=1), jnp.concatenate([tables[6 + q, 0], tables[6 + q, 0], tables[6 + q, 1]], axis=0)))
            halves = (backs[0] + backs[1], backs[0] - backs[1])
            for part in range(2):
                rows = part * half + chunk * CHUNK
                here = slice(rows, rows + CHUNK)
                total = [[0.0, 0.0], [0.0, 0.0]]
                for b in range(2):
                    xr = patch[0, b, here, :]
                    xi = patch[1, b, here, :]
                    for m in range(modes):
                        at = (2 * m + part) * CHUNK
                        br = halves[b][at : at + CHUNK, :half]
                        bi = halves[b][at : at + CHUNK, half:]
                        pr = probe[0, m, here, b * half : (b + 1) * half]
                        pi = probe[1, m, here, b * half : (b + 1) * half]
                        total[0][b] += pr * br + pi * bi
                        total[1][b] += pr * bi - pi * br
                        sums[((((b * 2 + 0) * modes + m) * length + rows) // piece_rows) ^ code, pl.ds(rows % piece_rows, CHUNK), :] += xr * br + xi * bi
                        sums[((((b * 2 + 1) * modes + m) * length + rows) // piece_rows) ^ code, pl.ds(rows % piece_rows, CHUNK), :] += xr * bi - xi * br
                for c in range(2):
                    ra = pltpu.roll(total[c][0], fore_shift, 1)
                    rb = pltpu.roll(total[c][1], fore_shift, 1)
                    beyond = lane >= shift
                    zero = jnp.zeros_like(ra)
                    placed = (jnp.where(beyond, ra, zero), jnp.where(beyond, rb, ra), jnp.where(beyond, zero, rb))
                    for b in range(3):
                        grid[c, block + b, pl.ds(row0 + rows, CHUNK), :] += placed[b]
        return carry

    lax.fori_loop(0, scalars[0], slot_step, 0)

    inner_side_out[...] = grid[:, inner]
    outer_side_out[...] = grid[:, outer]
    for b in range(2):
        grad_mid[:, :, b * half : (b + 1) * half] = grid[:, 1 + b]


def rows_kernel(grad_mid, inner_side, outer_side, _, core_out, chip_out, inner_grad):
    margin, length = core_out.shape[1], inner_grad.shape[1]
    near, far = (pl.ds(start, margin) for start in near_and_far(margin + length))
    for side, start in zip((inner_side, outer_side), inner_and_outer()):
        cols = pl.ds(start, LANES)
        for target, rows in ((core_out, near), (chip_out, far), (inner_grad, slice(margin, margin + length))):
            target[:, :, cols] = grad_mid[:, rows, cols] + side[:, rows, :]


def columns_kernel(inner_grad, core_in, chip_in, grad):
    near, far = (pl.ds(start, LANES) for start in near_and_far(LANES))
    grad[:, near, :] = inner_grad[:, near, :] + core_in[...]
    grad[:, far, :] = inner_grad[:, far, :] + chip_in[...]


def after_kernel(_, *refs):
    join_pieces(refs[:-1], refs[-1])


def join_pieces(pieces, joined):
    count = pieces[0].shape[0]
    for i, piece in enumerate(pieces):
        joined[i * count : (i + 1) * count] = piece[...]


def join_kernel(first, *refs):
    source, out, sems = refs[0], refs[-2], refs[-1]
    kept, rows, _ = source.shape
    _, modes, length, _ = out.shape
    code = own_code(digit_groups())
    each = length // rows
    copies = []
    for place in range(kept):
        piece = (place + first) ^ code
        row = pl.multiple_of(piece % each * rows, rows)
        m = piece // each % modes
        c = piece // (each * modes) % 2
        b = pl.multiple_of(piece // (each * modes * 2) * LANES, LANES)
        copies.append(
            pltpu.make_async_copy(source.at[place], out.at[c, m, pl.ds(row, rows), pl.ds(b, LANES)], sems.at[place])
        )
    for copy in copies:
        copy.start()
    for copy in copies:
        copy.wait()


def exchanged(value, axis, mask):
    return lax.ppermute(value, axis, [(i, i ^ mask) for i in range(lax.axis_size(axis))])


def digit_groups():
    groups = [("ty", [1])]
    bits = [1 << i for i in range(1, lax.axis_size("ty").bit_length() - 1)]
    groups += [("ty", bits[i : i + 2]) for i in range(0, len(bits), 2)]
    return groups + [("tx", [1])]


def masks(bits):
    return [sum(bit for i, bit in enumerate(reversed(bits)) if j >> i & 1) for j in range(1 << len(bits))]


def own_code(groups):
    code = 0
    for axis, bits in groups:
        index = lax.axis_index(axis)
        for bit in bits:
            code = code * 2 + (index // bit) % 2
    return code


def pair_partner(index, kind):
    return index ^ 1 if kind == "inner" else index + 1 if index % 2 else index - 1


def paired(value, axis, kind):
    count = lax.axis_size(axis)
    pairs = [(i, pair_partner(i, kind)) for i in range(count)]
    return lax.ppermute(value, axis, [(i, j) for i, j in pairs if 0 <= j < count])


def add_kernel(scale, own, *refs):
    others, out = refs[:-1], refs[-1]
    count = out.shape[0]
    total = own[:count]
    for other in others:
        total += other[...]
    out[...] = total * scale


def added(own, others, scale=1.0, weight=0):
    out = jax.ShapeDtypeStruct(others[0].shape, jnp.float32)
    (result,) = call(functools.partial(add_kernel, scale), "add", [out], (own, *others), weight=weight)
    return result


def scattered(value, axis, bits):
    places = masks(bits)
    count = value.shape[0] // len(places)
    return [exchanged(value[j * count : (j + 1) * count], axis, places[j]) for j in range(1, len(places))]


def gathered(value, axis, bits):
    return [value] + [exchanged(value, axis, mask) for mask in masks(bits)[1:]]


def call(body, name, out, operands, spaces="", results="", scratch=(), limit=SMALL_LIMIT, weight=0, aliases=None):
    kinds = {"v": pltpu.VMEM, "s": pltpu.SMEM, "h": pltpu.HBM}

    def specs(letters, count):
        return tuple(pl.BlockSpec(memory_space=kinds[x]) for x in letters + "v" * (count - len(letters)))

    moved = sum(math.prod(v.shape) * v.dtype.itemsize for v in tuple(operands) + tuple(out))
    return pl.pallas_call(
        body,
        out_shape=tuple(out),
        in_specs=specs(spaces, len(operands)),
        out_specs=specs(results, len(out)),
        scratch_shapes=list(scratch),
        input_output_aliases=aliases or {},
        compiler_params=pltpu.CompilerParams(vmem_limit_bytes=limit),
        cost_estimate=pl.CostEstimate(flops=weight, bytes_accessed=moved, transcendentals=0),
        name=name,
    )(*operands)


def shards(object_field, probe_modes, intensities, offsets, counts):
    length = object_field.shape[1]
    modes, pattern = probe_modes.shape[1:3]
    margin = pattern // 2
    half = LANES
    devices = lax.axis_size("ty") * lax.axis_size("tx")
    groups = digit_groups()
    f32, bf16 = jnp.float32, jnp.bfloat16
    slots = intensities.shape[2]
    tables = jnp.asarray(fourier_tables(pattern))

    def shape(*sizes):
        return jax.ShapeDtypeStruct(sizes, f32)

    tile, rows_shape = shape(2, length, length), shape(2, margin, length)
    side, tall_side, corner = shape(2, length, margin), shape(2, length + 2 * margin, margin), shape(2, margin, margin)
    core_tile = paired(object_field, "ty", "inner")
    (leaving,) = call(chip_edges_kernel, "chip_edges", [rows_shape], (object_field,), "h", scratch=(pltpu.SemaphoreType.DMA,))
    center, inner_side, outer_side = call(
        edges_kernel, "edges", [tile, side, side], (object_field, leaving), "hh", scratch=(pltpu.SemaphoreType.DMA((3,)),), weight=AROUND
    )
    chip_rows = leaving
    chip_rows = paired(chip_rows, "ty", "outer")
    inner_side = paired(inner_side, "tx", "inner")
    outer_side = paired(outer_side, "tx", "outer")
    (root,) = call(
        root_kernel,
        "root",
        [shape(slots, 2, half, pattern)],
        (intensities[0, 0],),
        scratch=(pltpu.VMEM((slots, 2, pattern, half), f32),),
        weight=AROUND,
    )
    (scalars,) = call(
        places_kernel, "places", [jax.ShapeDtypeStruct((1 + 2 * slots,), jnp.int32)], (counts.T, offsets[0, 0].T), "ss", "s", weight=AROUND
    )
    inner_corner, outer_corner = call(corners_kernel, "corners", [corner, corner], (chip_rows, root, scalars), "vhh")
    inner_corner = paired(inner_corner, "tx", "inner")
    outer_corner = paired(outer_corner, "tx", "outer")
    (near_corners,) = call(near_kernel, "near", [shape(2, 2, margin, margin)], (inner_side, outer_side))
    near_corners = paired(near_corners, "ty", "inner")
    (far_rows,) = call(far_kernel, "far", [shape(2, 4, margin, half)], (chip_rows, inner_corner, outer_corner), weight=AHEAD)
    pieces = 1 << sum(len(bits) for _, bits in groups)
    rows = 2 * 2 * modes * pattern // pieces
    value, inner_side, outer_side, grad_mid = call(
        slots_kernel,
        "slots",
        [shape(pieces, rows, half), tall_side, tall_side, shape(2, length + 2 * margin, length)],
        (
            scalars, center, core_tile, far_rows, inner_side, outer_side, near_corners,
            probe_modes, root, tables,
        ),
        "s",
        scratch=(
            pltpu.VMEM((2, 4, length + 2 * margin, half), f32),
            pltpu.VMEM((2, 4, length + 2 * margin, half), f32),
            pltpu.VMEM((2, 2, pattern, half), f32),
            pltpu.VMEM((modes, 2, pattern, pattern), bf16),
            pltpu.VMEM((modes, 2, pattern, pattern), bf16),
            pltpu.VMEM((modes, 2, pattern, pattern), f32),
        ),
        limit=VMEM_LIMIT,
    )

    value = added(value, [paired(value[pieces // 2 :], "ty", "inner")], weight=HEAVY)
    inner_side = paired(inner_side, "tx", "inner")
    outer_side = paired(outer_side, "tx", "outer")
    for group in groups[1:-1]:
        value = added(value, scattered(value, *group))
    value = added(value, scattered(value, *groups[-1]), scale=1.0 / devices)
    core_rows, chip_rows, inner_grad = call(
        rows_kernel,
        "rows",
        [rows_shape, rows_shape, tile],
        (grad_mid, inner_side, outer_side, value),
        "vvvh",
        weight=HEAVY,
    )
    chip_rows = paired(chip_rows, "ty", "outer")
    core_rows = paired(core_rows, "ty", "inner")
    for i in range(1, lax.axis_size("tx").bit_length() - 1):
        value = added(value, [exchanged(value, "tx", 1 << i)], weight=4000000000)
    for i in range(len(groups) - 1, 0, -1):
        parts = gathered(value, *groups[i])
        joined = shape(len(parts) * value.shape[0], rows, half)
        arrived = chip_rows if i == len(groups) - 1 else core_rows
        (value,) = call(after_kernel, "after", [joined], (arrived, *parts), "h", weight=4000000000)
    (object_grad,) = call(columns_kernel, "columns", [tile], (inner_grad, core_rows, chip_rows))
    other = paired(value, "ty", "inner")
    sems = (pltpu.SemaphoreType.DMA((pieces // 2,)),)
    (probe_grad,) = call(
        functools.partial(join_kernel, 0), "join", [shape(*probe_modes.shape)], (value,), "v", "h", sems, weight=AROUND
    )
    (probe_grad,) = call(
        functools.partial(join_kernel, pieces // 2),
        "join_rest",
        [shape(*probe_modes.shape)],
        (other, probe_grad),
        "vh",
        "h",
        sems,
        aliases={1: 0},
    )
    return (object_grad, probe_grad)


def solution(mesh):
    placed = (
        P(None, "ty", "tx"),
        P(),
        P("ty", "tx", None, None, None),
        P("ty", "tx", None, None),
        P(),
    )
    return jax.shard_map(
        shards, mesh=mesh, in_specs=placed, out_specs=(P(None, "ty", "tx"), P()), check_vma=False
    )
```
